256 devices in a mesh: gz: 4 (over y), xy: 64 (over z, x, core).
Axes of the slice: x: 4, y: 4, z: 8, core: 2. Of those that a mesh axis runs over, the one named last changes fastest.
Arguments:
- sections: bfloat16 [4, 8192, 1024], P('gz', 'xy'), may hold values from -6 to 6
- peak_offsets: int32 [2, 4, 64, 8], P(None, 'gz', 'xy'), may hold values from -2 to 2
- confidence: int32 [4, 64, 8], P('gz', 'xy'), may hold values from 1 to 4
- tissue_mask: int32 [4, 64, 8], P('gz', 'xy'), may hold values 0 or 1
Outputs:
- flow_field: float32 [2, 4, 64, 8], P(None, 'gz', 'xy')
- correction: float32 [2, 4, 64, 8], P(None, 'gz', 'xy')
The draws below stay inside these ranges and needn't reach their ends.
All inputs are finite; a program needn't handle non-finite values. No bound on the sum of `tissue_mask` on one device may be relied on, other than what follows from the above.
Results may differ from the reference program's by a relative error of at most 0.0003.
Values may be sent and summed in bfloat16 or wider, within the bound.
No kernel may reach another device: no remote copies, remote signals or barrier semaphores. Data moves between devices by JAX's collectives and lax.ppermute only.
A program may use at most 128 MiB of HBM per device.

```python
import jax
import jax.numpy as jnp
from jax import lax

PC = 8
PATCH = 128
ITERS = 4
NSEC = 4
NR = 64
HEIGHT = 8192
WIDTH = 1024


def plant(result, rng, low, largest):
    longest = result.shape.index(max(result.shape))
    spots = []
    for shift in (0, 1):
        where = [jax.random.randint(jax.random.fold_in(rng, axis), (), 0, length) for axis, length in enumerate(result.shape)]
        where[longest] = (where[longest] + shift) % result.shape[longest]
        spots.append(tuple(where))
    return result.at[spots[0]].set(low).at[spots[1]].set(largest)


def shard_levels(rng, shape, cuts, least, top_value):
    gain = 1.0
    for axis_at, parts in cuts:
        draws = jax.random.uniform(jax.random.fold_in(jax.random.fold_in(rng, 6), axis_at), (parts,), jnp.float32, least / len(cuts), top_value / len(cuts))
        gain = gain * jnp.repeat(jnp.exp(draws), shape[axis_at] // parts).reshape((-1,) + (1,) * (len(shape) - 1 - axis_at))
    return gain


def scatter_about(key, dims, width, bound, shards=(), kind=jnp.bfloat16):
    array = jax.random.normal(key, dims, jnp.float32) * width
    if len(shards) > 0:
        array = shard_levels(key, dims, shards, -0.22, 0.18) * array
    return jnp.clip(array, min=-bound, max=bound).astype(kind)


def setup_inputs(seed: int = 0) -> dict:
    seeds = jax.random.split(jax.random.key(seed), 5)
    return {
        "sections": scatter_about(seeds[0], (NSEC, HEIGHT, WIDTH), 1.0, 6.0, ((0, 4), (1, 64))),
        "peak_offsets": plant(jax.random.randint(seeds[1], (2, NSEC, NR, PC), 0 - 2, 3), jax.random.fold_in(seeds[1], 1), 0 - 2, 2).astype(jnp.int32),
        "confidence": plant(jax.random.randint(seeds[2], (NSEC, NR, PC), 1, 5), jax.random.fold_in(seeds[2], 1), 1, 4).astype(jnp.int32),
        "tissue_mask": plant((jax.random.randint(seeds[3], (NSEC, NR, PC), 0, 4) < 3).astype(jnp.int32), jax.random.fold_in(seeds[3], 1), 0, 1),
    }


STEP_SIZE = 0.12


def score_table(current, previous):
    rows = current.shape[0] // PATCH
    columns = current.shape[1] // PATCH
    moving = current.reshape(rows, PATCH, columns, PATCH)
    fixed_img = previous.reshape(rows, PATCH, columns, PATCH).astype(jnp.float32)
    tables = []
    for shift_y in range(-3, 4):
        rolled_y = jnp.roll(moving, -shift_y, axis=1)
        for shift_x in range(-3, 4):
            window = jnp.roll(rolled_y, -shift_x, axis=3).astype(jnp.float32)
            tables.append(jnp.sum(fixed_img * window, axis=(1, 3)) / PATCH)
    return jnp.stack(tables).reshape(7, 7, rows, columns)


def pick_score(table, want_y, want_x):
    levels = jnp.arange(7, dtype=jnp.int32) - 3
    hit_y = (levels[:, None, None] == want_y[None]).astype(jnp.float32)
    hit_x = (levels[:, None, None] == want_x[None]).astype(jnp.float32)
    return jnp.sum(table * hit_y[:, None] * hit_x[None], axis=(0, 1))


def correlate(current, previous, peak):
    table = score_table(current, previous)
    center = pick_score(table, peak[0], peak[1])
    y_plus = pick_score(table, peak[0] + 1, peak[1])
    y_minus = pick_score(table, peak[0] - 1, peak[1])
    x_plus = pick_score(table, peak[0], peak[1] + 1)
    x_minus = pick_score(table, peak[0], peak[1] - 1)
    delta_y = (y_plus - y_minus) / (jnp.abs(y_minus) + jnp.abs(center) + jnp.abs(y_plus) + 1.0)
    delta_x = (x_plus - x_minus) / (jnp.abs(x_minus) + jnp.abs(center) + jnp.abs(x_plus) + 1.0)
    return jnp.stack([delta_y, delta_x])


def relax_force(nodes, padded_z, padded_rows, has_up, has_down, stiffness, next_stiff, flow_field, next_flow):
    force = jnp.where(has_up[None, None, :, None], padded_rows[:, :, :-2] - nodes, 0.0)
    force = force + jnp.where(has_down[None, None, :, None], padded_rows[:, :, 2:] - nodes, 0.0)
    zero_col = jnp.zeros(nodes.shape[:3] + (1,), jnp.float32)
    force = force + jnp.concatenate([zero_col, nodes[..., :-1] - nodes[..., 1:]], axis=3)
    force = force + jnp.concatenate([nodes[..., 1:] - nodes[..., :-1], zero_col], axis=3)
    force = force + stiffness[None] * (padded_z[:, :-2] + flow_field - nodes)
    force = force + next_stiff[None] * (padded_z[:, 2:] - next_flow - nodes)
    return force


def reference(sections, peak_offsets, confidence, tissue_mask):
    count = sections.shape[0]

    def one_section(index):
        current = sections[index]
        previous = sections[jnp.maximum(index - 1, 0)]
        previous = jnp.where(index > 0, previous, jnp.zeros_like(previous))
        return correlate(current, previous, peak_offsets[:, index])

    deltas = lax.map(one_section, jnp.arange(count, dtype=jnp.int32))
    flow_field = peak_offsets.astype(jnp.float32) + jnp.transpose(deltas, (1, 0, 2, 3))
    order = jnp.arange(count, dtype=jnp.int32)
    stiffness = confidence.astype(jnp.float32) * 0.25 * tissue_mask.astype(jnp.float32)
    stiffness = stiffness * (order > 0).astype(jnp.float32)[:, None, None]
    start = jnp.cumsum(flow_field, axis=1)
    nodes = start
    next_stiff = jnp.concatenate([stiffness[1:], jnp.zeros_like(stiffness[:1])], axis=0)
    next_flow = jnp.concatenate([flow_field[:, 1:], jnp.zeros_like(flow_field[:, :1])], axis=1)
    row_ids = jnp.arange(nodes.shape[2], dtype=jnp.int32)
    has_up = row_ids > 0
    has_down = row_ids < nodes.shape[2] - 1
    for iteration in range(ITERS):
        padded_z = jnp.pad(nodes, ((0, 0), (1, 1), (0, 0), (0, 0)))
        padded_rows = jnp.pad(nodes, ((0, 0), (0, 0), (1, 1), (0, 0)))
        force = relax_force(nodes, padded_z, padded_rows, has_up, has_down, stiffness, next_stiff, flow_field, next_flow)
        nodes = nodes + STEP_SIZE * force
    return flow_field, nodes - start
```

```python
import jax
import jax.numpy as jnp
from jax import lax
from jax.experimental import pallas as pl
from jax.experimental.pallas import tpu as pltpu
from jax.sharding import PartitionSpec as P

PATCH = 128
LANES = 128
COLS = 8
ITERS = 4
STEP_SIZE = 0.12
PLANE = 8


def place():
    gz = lax.axis_index("gz")
    xy = lax.axis_index("xy")
    return gz, xy


def correlate_kernel(pk_ref, own_ref, got_ref, peak_ref, conf_ref, mask_ref, out_ref, pad_ref):
    gz, xy = place()
    odd = lax.rem(xy, 2)
    sign = 1 - 2 * odd
    target = gz + odd
    sums = []
    for j in range(COLS):
        cols = slice(j * PATCH, (j + 1) * PATCH)
        own = own_ref[0, :, cols].astype(jnp.float32)
        got = got_ref[0, :, cols].astype(jnp.float32)
        shift_y = -sign * pk_ref[0, 0, 0, j]
        shift_x = -sign * pk_ref[1, 0, 0, j]
        moved = pltpu.roll(own, lax.rem(shift_x + PATCH, PATCH), 1)
        pad_ref[j, 8 : 8 + PATCH, :] = moved
        pad_ref[j, 0:8, :] = moved[PATCH - 8 :, :]
        pad_ref[j, 8 + PATCH :, :] = moved[0:8, :]
        center = pad_ref[j, pl.ds(8 - shift_y, PATCH), :]
        windows = (
            center,
            pad_ref[j, pl.ds(9 - shift_y, PATCH), :],
            pad_ref[j, pl.ds(7 - shift_y, PATCH), :],
            pltpu.roll(center, PATCH - 1, 1),
            pltpu.roll(center, 1, 1),
        )
        sums.append(
            [
                jnp.sum(jnp.sum((w * got).reshape(PATCH // 8, 8, LANES), axis=0), axis=0, keepdims=True)
                for w in windows
            ]
        )
    scores = []
    for k in range(5):
        stacked = jnp.concatenate([sums[j][k] for j in range(COLS)], axis=0)
        scores.append(jnp.sum(stacked, axis=1, keepdims=True) * (1.0 / PATCH))
    center, y_plus, y_minus, x_plus, x_minus = scores
    paired = jnp.logical_and(target > 0, target < 4)
    scale = jnp.where(paired, sign, 0).astype(jnp.float32)
    delta_y = scale * (y_plus - y_minus) / (jnp.abs(y_minus) + jnp.abs(center) + jnp.abs(y_plus) + 1.0)
    delta_x = scale * (x_plus - x_minus) / (jnp.abs(x_minus) + jnp.abs(center) + jnp.abs(x_plus) + 1.0)
    lane = lax.broadcasted_iota(jnp.int32, (COLS, LANES), 1)
    patch = lax.broadcasted_iota(jnp.int32, (COLS, LANES), 0)
    spread = jnp.where(lane == target * 16 + patch, delta_y, 0.0)
    spread = spread + jnp.where(lane == target * 16 + COLS + patch, delta_x, 0.0)
    row = jnp.sum(spread, axis=0, keepdims=True)
    stiff = conf_ref[0].astype(jnp.float32) * 0.25 * mask_ref[0].astype(jnp.float32)
    stiff = stiff * (gz > 0).astype(jnp.float32)
    gap = jnp.zeros((1, 48), jnp.float32)
    fixed = jnp.concatenate(
        [
            peak_ref[0, 0].astype(jnp.float32),
            peak_ref[1, 0].astype(jnp.float32),
            gap,
            stiff,
            stiff,
            gap,
        ],
        axis=1,
    )
    row = row + pltpu.roll(fixed, gz * 16, 1)
    out_ref[...] = jnp.broadcast_to(row[None], out_ref.shape)


def relax_kernel(own_ref, got_ref, flow_ref, corr_ref):
    gz, xy = place()
    z = xy // PLANE
    inner = lax.rem(xy, PLANE)
    upper = inner < PLANE // 2

    def folded(ref):
        parts = [ref[g * PLANE : (g + 1) * PLANE, 0, :] for g in range(4)]
        return (parts[0] + parts[1]) + (parts[2] + parts[3])

    own = folded(own_ref)
    got = folded(got_ref)
    window = jnp.concatenate([jnp.where(upper, got, own), jnp.where(upper, own, got)], axis=0)
    base = jnp.where(upper, z - 1, z) * PLANE
    here = jnp.where(upper, PLANE + inner, inner)
    shape = (2 * PLANE, LANES)
    lane = lax.broadcasted_iota(jnp.int32, shape, 1)
    local = lax.broadcasted_iota(jnp.int32, shape, 0)
    row = local + base
    col = lax.rem(lane, COLS)
    has_up = row > 0
    has_down = row < 63
    has_left = col > 0
    has_right = col < COLS - 1
    flow = jnp.where(lane < 64, window, 0.0)
    stiff = jnp.where(lane < 64, pltpu.roll(window, 64, 1), 0.0)
    next_stiff = jnp.where(lane < 48, pltpu.roll(stiff, LANES - 16, 1), 0.0)
    next_flow = jnp.where(lane < 48, pltpu.roll(flow, LANES - 16, 1), 0.0)
    start = flow + jnp.where(lane >= 16, pltpu.roll(flow, 16, 1), 0.0)
    start = start + jnp.where(lane >= 32, pltpu.roll(start, 32, 1), 0.0)
    nodes = start
    for _ in range(ITERS):
        force = jnp.where(has_up, pltpu.roll(nodes, 1, 0) - nodes, 0.0)
        force = force + jnp.where(has_down, pltpu.roll(nodes, 2 * PLANE - 1, 0) - nodes, 0.0)
        force = force + jnp.where(has_left, pltpu.roll(nodes, 1, 1) - nodes, 0.0)
        force = force + jnp.where(has_right, pltpu.roll(nodes, LANES - 1, 1) - nodes, 0.0)
        force = force + stiff * (pltpu.roll(nodes, 16, 1) + flow - nodes)
        force = force + next_stiff * (pltpu.roll(nodes, LANES - 16, 1) - next_flow - nodes)
        nodes = nodes + STEP_SIZE * force
    turn = lax.rem(LANES - gz * 16, LANES)
    for value, ref in ((flow, flow_ref), (nodes - start, corr_ref)):
        mine = jnp.sum(jnp.where(local == here, value, 0.0), axis=0, keepdims=True)
        mine = pltpu.roll(mine, turn, 1)
        ref[0, 0] = mine[:, 0:COLS]
        ref[1, 0] = mine[:, COLS : 2 * COLS]


def on_device(sections, peak_offsets, confidence, tissue_mask):
    groups = lax.axis_size("gz")
    strips = lax.axis_size("xy")
    swap = []
    fetch = []
    for strip in range(strips):
        for group in range(groups):
            this = group * strips + strip
            after = (group + 1) % groups * strips + strip
            swap.append((this, after) if strip % 2 == 0 else (after, this))
            fetch.append((this, this) if strip % 2 == 0 else (after, this))
    got = lax.ppermute(sections, ("gz", "xy"), swap)
    peaks = lax.ppermute(peak_offsets, ("gz", "xy"), fetch)
    vmem = pl.BlockSpec(memory_space=pltpu.VMEM)
    smem = pl.BlockSpec(memory_space=pltpu.SMEM)
    row = pl.pallas_call(
        correlate_kernel,
        out_shape=jax.ShapeDtypeStruct((32, 1, LANES), jnp.float32),
        in_specs=[smem, vmem, vmem, vmem, vmem, vmem],
        out_specs=vmem,
        scratch_shapes=[pltpu.VMEM((COLS, PATCH + 16, LANES), jnp.float32)],
    )(peaks, sections, got, peak_offsets, confidence, tissue_mask)
    planes = [
        [group * strips + plane * PLANE + inner for group in range(groups) for inner in range(PLANE)]
        for plane in range(strips // PLANE)
    ]
    block = lax.all_to_all(row, ("gz", "xy"), 0, 0, axis_index_groups=planes, tiled=True)
    hop = []
    for device in range(groups * strips):
        group, strip = divmod(device, strips)
        step = PLANE if strip % PLANE < PLANE // 2 else -PLANE
        hop.append((device, group * strips + (strip + step) % strips))
    beside = lax.ppermute(block, ("gz", "xy"), hop)
    shape = jax.ShapeDtypeStruct(peak_offsets.shape, jnp.float32)
    return pl.pallas_call(
        relax_kernel,
        out_shape=(shape, shape),
        in_specs=[vmem, vmem],
        out_specs=(vmem, vmem),
    )(block, beside)


def solution(mesh):
    in_specs = (
        P("gz", "xy", None),
        P(None, "gz", "xy", None),
        P("gz", "xy", None),
        P("gz", "xy", None),
    )
    out_specs = (P(None, "gz", "xy", None), P(None, "gz", "xy", None))
    return jax.shard_map(
        on_device, mesh=mesh, in_specs=in_specs, out_specs=out_specs, check_vma=False
    )
```

```python
import jax
import jax.numpy as jnp
from jax import lax
from jax.experimental import pallas as pl
from jax.experimental.pallas import tpu as pltpu
from jax.sharding import PartitionSpec as P

PATCH = 128
LANES = 128
COLS = 8
ITERS = 4
STEP_SIZE = 0.12
PLANE = 8
REACH = 3
EDGE = 8
MIB = 1024 * 1024


def place():
    gz = lax.axis_index("gz")
    xy = lax.axis_index("xy")
    return gz, xy


def prepare_kernel(own_ref, conf_ref, mask_ref, shifted_ref, stiff_ref):
    for j in range(COLS):
        own = own_ref[0, :, j * PATCH : (j + 1) * PATCH].astype(jnp.float32)
        for v in range(2 * REACH + 1):
            moved = own if v == REACH else pltpu.roll(own, (REACH - v) % PATCH, 1)
            shifted_ref[v, j, EDGE : EDGE + PATCH, :] = moved
            shifted_ref[v, j, 0:EDGE, :] = moved[PATCH - EDGE :, :]
            shifted_ref[v, j, EDGE + PATCH :, :] = moved[0:EDGE, :]
    gz, _ = place()
    stiff = conf_ref[0].astype(jnp.float32) * 0.25 * mask_ref[0].astype(jnp.float32)
    stiff = stiff * (gz > 0).astype(jnp.float32)
    gap = jnp.zeros((1, 48), jnp.float32)
    stiff = jnp.concatenate([gap, gap[:, :16], stiff, stiff, gap], axis=1)
    stiff_ref[...] = pltpu.roll(stiff, gz * 16, 1)


def correlate_kernel(shifted_ref, got_ref, peak_ref, stiff_ref, out_ref):
    gz, xy = place()
    odd = lax.rem(xy, 2)
    sign = 1 - 2 * odd
    target = lax.rem(gz + odd, 4)
    peaks = [peak_ref[0, 0], peak_ref[1, 0]]
    sums = []
    for j in range(COLS):
        got = got_ref[0, :, j * PATCH : (j + 1) * PATCH].astype(jnp.float32)
        down = EDGE + sign * peaks[0][0, j]
        right = REACH + sign * peaks[1][0, j]
        sums.append(
            [
                jnp.sum(
                    jnp.sum(
                        (shifted_ref[right + v, j, pl.ds(down + u, PATCH), :] * got).reshape(
                            PATCH // 8, 8, LANES
                        ),
                        axis=0,
                    ),
                    axis=0,
                    keepdims=True,
                )
                for u, v in ((0, 0), (1, 0), (-1, 0), (0, 1), (0, -1))
            ]
        )
    scores = []
    for k in range(5):
        stacked = jnp.concatenate([sums[j][k] for j in range(COLS)], axis=0)
        scores.append(jnp.sum(stacked, axis=1, keepdims=True) * (1.0 / PATCH))
    center, y_plus, y_minus, x_plus, x_minus = scores
    scale = jnp.where(target > 0, sign, 0).astype(jnp.float32)
    delta_y = scale * (y_plus - y_minus) / (jnp.abs(y_minus) + jnp.abs(center) + jnp.abs(y_plus) + 1.0)
    delta_x = scale * (x_plus - x_minus) / (jnp.abs(x_minus) + jnp.abs(center) + jnp.abs(x_plus) + 1.0)
    lane = lax.broadcasted_iota(jnp.int32, (COLS, LANES), 1)
    patch = lax.broadcasted_iota(jnp.int32, (COLS, LANES), 0)
    spread = jnp.where(lane == patch, delta_y, 0.0)
    spread = spread + jnp.where(lane == COLS + patch, delta_x, 0.0)
    gap = jnp.zeros((1, LANES - 2 * COLS), jnp.float32)
    flow = [peaks[0].astype(jnp.float32), peaks[1].astype(jnp.float32), gap]
    flow = jnp.concatenate(flow, axis=1) + jnp.sum(spread, axis=0, keepdims=True)
    row = stiff_ref[...] + pltpu.roll(flow, target * 16, 1)
    out_ref[...] = jnp.broadcast_to(row[None], out_ref.shape)


def relax_kernel(own_ref, got_ref, flow_ref, corr_ref):
    gz, xy = place()
    z = xy // PLANE
    inner = lax.rem(xy, PLANE)
    upper = inner < PLANE // 2

    def folded(ref):
        parts = [ref[g * PLANE : (g + 1) * PLANE, 0, :] for g in range(4)]
        return (parts[0] + parts[1]) + (parts[2] + parts[3])

    own = folded(own_ref)
    got = folded(got_ref)
    window = jnp.concatenate([jnp.where(upper, got, own), jnp.where(upper, own, got)], axis=0)
    base = jnp.where(upper, z - 1, z) * PLANE
    here = jnp.where(upper, PLANE + inner, inner)
    shape = (2 * PLANE, LANES)
    lane = lax.broadcasted_iota(jnp.int32, shape, 1)
    local = lax.broadcasted_iota(jnp.int32, shape, 0)
    row = local + base
    col = lax.rem(lane, COLS)
    has_up = row > 0
    has_down = row < 63
    has_left = col > 0
    has_right = col < COLS - 1
    flow = jnp.where(lane < 64, window, 0.0)
    stiff = jnp.where(lane < 64, pltpu.roll(window, 64, 1), 0.0)
    next_stiff = jnp.where(lane < 48, pltpu.roll(stiff, LANES - 16, 1), 0.0)
    next_flow = jnp.where(lane < 48, pltpu.roll(flow, LANES - 16, 1), 0.0)
    start = flow + jnp.where(lane >= 16, pltpu.roll(flow, 16, 1), 0.0)
    start = start + jnp.where(lane >= 32, pltpu.roll(start, 32, 1), 0.0)
    nodes = start
    for _ in range(ITERS):
        force = jnp.where(has_up, pltpu.roll(nodes, 1, 0) - nodes, 0.0)
        force = force + jnp.where(has_down, pltpu.roll(nodes, 2 * PLANE - 1, 0) - nodes, 0.0)
        force = force + jnp.where(has_left, pltpu.roll(nodes, 1, 1) - nodes, 0.0)
        force = force + jnp.where(has_right, pltpu.roll(nodes, LANES - 1, 1) - nodes, 0.0)
        force = force + stiff * (pltpu.roll(nodes, 16, 1) + flow - nodes)
        force = force + next_stiff * (pltpu.roll(nodes, LANES - 16, 1) - next_flow - nodes)
        nodes = nodes + STEP_SIZE * force
    turn = lax.rem(LANES - gz * 16, LANES)
    for value, ref in ((flow, flow_ref), (nodes - start, corr_ref)):
        mine = jnp.sum(jnp.where(local == here, value, 0.0), axis=0, keepdims=True)
        mine = pltpu.roll(mine, turn, 1)
        ref[0, 0] = mine[:, 0:COLS]
        ref[1, 0] = mine[:, COLS : 2 * COLS]


def routes(groups, strips):
    half = PLANE // 2
    last = strips // PLANE - 1
    swap, fetch, hop = [], [], []
    for group in range(groups):
        for strip in range(strips):
            this = group * strips + strip
            if strip % 2 == 0:
                swap.append((this, this + strips if group < groups - 1 else this + 1))
                fetch.append((this, this))
            else:
                swap.append((this, this - strips if group > 0 else this - 1))
                fetch.append((this, (group - 1) % groups * strips + strip))
            plane, inner = divmod(strip, PLANE)
            if inner < half:
                hop.append((this, this + PLANE if plane < last else this + half))
            else:
                hop.append((this, this - PLANE if plane > 0 else this - half))
    return swap, fetch, hop


def on_device(sections, peak_offsets, confidence, tissue_mask):
    groups = lax.axis_size("gz")
    strips = lax.axis_size("xy")
    swap, fetch, hop = routes(groups, strips)
    got = lax.ppermute(sections, ("gz", "xy"), swap)
    peaks = lax.ppermute(peak_offsets, ("gz", "xy"), fetch)
    vmem = pl.BlockSpec(memory_space=pltpu.VMEM)
    shifted, stiff = pl.pallas_call(
        prepare_kernel,
        out_shape=(
            jax.ShapeDtypeStruct((2 * REACH + 1, COLS, PATCH + 2 * EDGE, LANES), jnp.float32),
            jax.ShapeDtypeStruct((1, LANES), jnp.float32),
        ),
        in_specs=[vmem, vmem, vmem],
        out_specs=(vmem, vmem),
        compiler_params=pltpu.CompilerParams(vmem_limit_bytes=8 * MIB),
    )(sections, confidence, tissue_mask)
    row = pl.pallas_call(
        correlate_kernel,
        out_shape=jax.ShapeDtypeStruct((32, 1, LANES), jnp.float32),
        in_specs=[vmem, vmem, vmem, vmem],
        out_specs=vmem,
        compiler_params=pltpu.CompilerParams(vmem_limit_bytes=8 * MIB),
    )(shifted, got, peaks, stiff)
    planes = [
        [group * strips + plane * PLANE + inner for group in range(groups) for inner in range(PLANE)]
        for plane in range(strips // PLANE)
    ]
    block = lax.all_to_all(row, ("gz", "xy"), 0, 0, axis_index_groups=planes, tiled=True)
    beside = lax.ppermute(block, ("gz", "xy"), hop)
    shape = jax.ShapeDtypeStruct(peak_offsets.shape, jnp.float32)
    return pl.pallas_call(
        relax_kernel,
        out_shape=(shape, shape),
        in_specs=[vmem, vmem],
        out_specs=(vmem, vmem),
        compiler_params=pltpu.CompilerParams(vmem_limit_bytes=4 * MIB),
    )(block, beside)


def solution(mesh):
    in_specs = (
        P("gz", "xy", None),
        P(None, "gz", "xy", None),
        P("gz", "xy", None),
        P("gz", "xy", None),
    )
    out_specs = (P(None, "gz", "xy", None), P(None, "gz", "xy", None))
    return jax.shard_map(
        on_device, mesh=mesh, in_specs=in_specs, out_specs=out_specs, check_vma=False
    )
```

```python
import jax
import jax.numpy as jnp
from jax import lax
from jax.experimental import pallas as pl
from jax.experimental.pallas import tpu as pltpu
from jax.sharding import PartitionSpec as P

PATCH = 128
LANES = 128
COLS = 8
ITERS = 4
STEP_SIZE = 0.12
PLANE = 8
REACH = 3
EDGE = 8
MIB = 1024 * 1024


def place():
    gz = lax.axis_index("gz")
    xy = lax.axis_index("xy")
    return gz, xy


def prepare_kernel(own_ref, peak_ref, conf_ref, mask_ref, shifted_ref, stiff_ref, kept_ref):
    kept_ref[...] = peak_ref[...]
    for j in range(COLS):
        own = own_ref[0, :, j * PATCH : (j + 1) * PATCH].astype(jnp.float32)
        for v in range(2 * REACH + 1):
            moved = own if v == REACH else pltpu.roll(own, (REACH - v) % PATCH, 1)
            shifted_ref[v, j, EDGE : EDGE + PATCH, :] = moved
            shifted_ref[v, j, 0:EDGE, :] = moved[PATCH - EDGE :, :]
            shifted_ref[v, j, EDGE + PATCH :, :] = moved[0:EDGE, :]
    gz, _ = place()
    stiff = conf_ref[0].astype(jnp.float32) * 0.25 * mask_ref[0].astype(jnp.float32)
    stiff = stiff * (gz > 0).astype(jnp.float32)
    gap = jnp.zeros((1, 48), jnp.float32)
    stiff = jnp.concatenate([gap, gap[:, :16], stiff, stiff, gap], axis=1)
    stiff_ref[...] = pltpu.roll(stiff, gz * 16, 1)


def correlate_kernel(shifted_ref, got_ref, kept_ref, sent_ref, stiff_ref, out_ref):
    gz, xy = place()
    odd = lax.rem(xy, 2)
    sign = 1 - 2 * odd
    target = lax.rem(gz + odd, 4)
    peaks = [jnp.where(odd > 0, sent_ref[i, 0], kept_ref[i, 0]) for i in range(2)]
    sums = []
    for j in range(COLS):
        got = got_ref[0, :, j * PATCH : (j + 1) * PATCH].astype(jnp.float32)
        down = EDGE + sign * peaks[0][0, j]
        right = REACH + sign * peaks[1][0, j]
        sums.append(
            [
                jnp.sum(
                    jnp.sum(
                        (shifted_ref[right + v, j, pl.ds(down + u, PATCH), :] * got).reshape(
                            PATCH // 8, 8, LANES
                        ),
                        axis=0,
                    ),
                    axis=0,
                    keepdims=True,
                )
                for u, v in ((0, 0), (1, 0), (-1, 0), (0, 1), (0, -1))
            ]
        )
    scores = []
    for k in range(5):
        stacked = jnp.concatenate([sums[j][k] for j in range(COLS)], axis=0)
        scores.append(jnp.sum(stacked, axis=1, keepdims=True) * (1.0 / PATCH))
    center, y_plus, y_minus, x_plus, x_minus = scores
    scale = jnp.where(target > 0, sign, 0).astype(jnp.float32)
    delta_y = scale * (y_plus - y_minus) / (jnp.abs(y_minus) + jnp.abs(center) + jnp.abs(y_plus) + 1.0)
    delta_x = scale * (x_plus - x_minus) / (jnp.abs(x_minus) + jnp.abs(center) + jnp.abs(x_plus) + 1.0)
    lane = lax.broadcasted_iota(jnp.int32, (COLS, LANES), 1)
    patch = lax.broadcasted_iota(jnp.int32, (COLS, LANES), 0)
    spread = jnp.where(lane == patch, delta_y, 0.0)
    spread = spread + jnp.where(lane == COLS + patch, delta_x, 0.0)
    gap = jnp.zeros((1, LANES - 2 * COLS), jnp.float32)
    flow = [peaks[0].astype(jnp.float32), peaks[1].astype(jnp.float32), gap]
    flow = jnp.concatenate(flow, axis=1) + jnp.sum(spread, axis=0, keepdims=True)
    row = stiff_ref[...] + pltpu.roll(flow, target * 16, 1)
    out_ref[...] = jnp.broadcast_to(row[None], out_ref.shape)


def relax_kernel(own_ref, got_ref, flow_ref, corr_ref):
    gz, xy = place()
    z = xy // PLANE
    inner = lax.rem(xy, PLANE)
    upper = inner < PLANE // 2

    own = own_ref[...]
    got = got_ref[...]
    window = jnp.concatenate([jnp.where(upper, got, own), jnp.where(upper, own, got)], axis=0)
    base = jnp.where(upper, z - 1, z) * PLANE
    here = jnp.where(upper, PLANE + inner, inner)
    shape = (2 * PLANE, LANES)
    lane = lax.broadcasted_iota(jnp.int32, shape, 1)
    local = lax.broadcasted_iota(jnp.int32, shape, 0)
    row = local + base
    col = lax.rem(lane, COLS)
    has_up = row > 0
    has_down = row < 63
    has_left = col > 0
    has_right = col < COLS - 1
    flow = jnp.where(lane < 64, window, 0.0)
    stiff = jnp.where(lane < 64, pltpu.roll(window, 64, 1), 0.0)
    next_stiff = jnp.where(lane < 48, pltpu.roll(stiff, LANES - 16, 1), 0.0)
    next_flow = jnp.where(lane < 48, pltpu.roll(flow, LANES - 16, 1), 0.0)
    start = flow + jnp.where(lane >= 16, pltpu.roll(flow, 16, 1), 0.0)
    start = start + jnp.where(lane >= 32, pltpu.roll(start, 32, 1), 0.0)
    nodes = start
    for _ in range(ITERS):
        force = jnp.where(has_up, pltpu.roll(nodes, 1, 0) - nodes, 0.0)
        force = force + jnp.where(has_down, pltpu.roll(nodes, 2 * PLANE - 1, 0) - nodes, 0.0)
        force = force + jnp.where(has_left, pltpu.roll(nodes, 1, 1) - nodes, 0.0)
        force = force + jnp.where(has_right, pltpu.roll(nodes, LANES - 1, 1) - nodes, 0.0)
        force = force + stiff * (pltpu.roll(nodes, 16, 1) + flow - nodes)
        force = force + next_stiff * (pltpu.roll(nodes, LANES - 16, 1) - next_flow - nodes)
        nodes = nodes + STEP_SIZE * force
    turn = lax.rem(LANES - gz * 16, LANES)
    for value, ref in ((flow, flow_ref), (nodes - start, corr_ref)):
        mine = jnp.sum(jnp.where(local == here, value, 0.0), axis=0, keepdims=True)
        mine = pltpu.roll(mine, turn, 1)
        ref[0, 0] = mine[:, 0:COLS]
        ref[1, 0] = mine[:, COLS : 2 * COLS]


def routes(groups, strips):
    last = strips // PLANE - 1
    swap, fetch, hop = [], [], []
    for group in range(groups):
        for strip in range(strips):
            this = group * strips + strip
            if strip % 2 == 0:
                swap.append((this, this + strips if group < groups - 1 else this + 1))
                fetch.append((this, group * strips + (strip ^ 2)))
            else:
                swap.append((this, this - strips if group > 0 else this - 1))
                fetch.append((this, (group - 1) % groups * strips + strip))
            plane, inner = divmod(strip, PLANE)
            twin = this ^ 1
            turn = this - inner + PLANE - 2 - inner // 2 * 2 + inner % 2
            if inner < PLANE // 2:
                hop.append((this, twin + PLANE if plane < last else turn))
            else:
                hop.append((this, twin - PLANE if plane > 0 else turn))
    return swap, fetch, hop


def on_device(sections, peak_offsets, confidence, tissue_mask):
    groups = lax.axis_size("gz")
    strips = lax.axis_size("xy")
    swap, fetch, hop = routes(groups, strips)
    got = lax.ppermute(sections, ("gz", "xy"), swap)
    sent = lax.ppermute(peak_offsets, ("gz", "xy"), fetch)
    vmem = pl.BlockSpec(memory_space=pltpu.VMEM)
    shifted, stiff, kept = pl.pallas_call(
        prepare_kernel,
        out_shape=(
            jax.ShapeDtypeStruct((2 * REACH + 1, COLS, PATCH + 2 * EDGE, LANES), jnp.float32),
            jax.ShapeDtypeStruct((1, LANES), jnp.float32),
            jax.ShapeDtypeStruct(peak_offsets.shape, jnp.int32),
        ),
        in_specs=[vmem, vmem, vmem, vmem],
        out_specs=(vmem, vmem, vmem),
        compiler_params=pltpu.CompilerParams(vmem_limit_bytes=8 * MIB),
    )(sections, peak_offsets, confidence, tissue_mask)
    row = pl.pallas_call(
        correlate_kernel,
        out_shape=jax.ShapeDtypeStruct((32, 1, LANES), jnp.float32),
        in_specs=[vmem, vmem, vmem, vmem, vmem],
        out_specs=vmem,
        compiler_params=pltpu.CompilerParams(vmem_limit_bytes=8 * MIB),
    )(shifted, got, kept, sent, stiff)
    planes = [
        [group * strips + plane * PLANE + inner for group in range(groups) for inner in range(PLANE)]
        for plane in range(strips // PLANE)
    ]
    block = lax.all_to_all(row, ("gz", "xy"), 0, 0, axis_index_groups=planes, tiled=True)
    block = jnp.sum(block.reshape(groups, PLANE, LANES), axis=0)
    beside = lax.ppermute(block, ("gz", "xy"), hop)
    shape = jax.ShapeDtypeStruct(peak_offsets.shape, jnp.float32)
    return pl.pallas_call(
        relax_kernel,
        out_shape=(shape, shape),
        in_specs=[vmem, vmem],
        out_specs=(vmem, vmem),
        compiler_params=pltpu.CompilerParams(vmem_limit_bytes=4 * MIB),
    )(block, beside)


def solution(mesh):
    in_specs = (
        P("gz", "xy", None),
        P(None, "gz", "xy", None),
        P("gz", "xy", None),
        P("gz", "xy", None),
    )
    out_specs = (P(None, "gz", "xy", None), P(None, "gz", "xy", None))
    return jax.shard_map(
        on_device, mesh=mesh, in_specs=in_specs, out_specs=out_specs, check_vma=False
    )
```

```python
import jax
import jax.numpy as jnp
from jax import lax
from jax.experimental import pallas as pl
from jax.experimental.pallas import tpu as pltpu
from jax.sharding import PartitionSpec as P

PATCH = 128
LANES = 128
COLS = 8
ITERS = 4
STEP_SIZE = 0.12
PLANE = 8
REACH = 3
EDGE = 8
MIB = 1024 * 1024


def place():
    gz = lax.axis_index("gz")
    xy = lax.axis_index("xy")
    return gz, xy


def prepare_kernel(own_ref, peak_ref, conf_ref, mask_ref, shifted_ref, stiff_ref, kept_ref):
    kept_ref[...] = peak_ref[...]
    for j in range(COLS):
        own = own_ref[0, :, j * PATCH : (j + 1) * PATCH].astype(jnp.float32)
        for v in range(2 * REACH + 1):
            moved = own if v == REACH else pltpu.roll(own, (REACH - v) % PATCH, 1)
            shifted_ref[v, j, EDGE : EDGE + PATCH, :] = moved
            shifted_ref[v, j, 0:EDGE, :] = moved[PATCH - EDGE :, :]
            shifted_ref[v, j, EDGE + PATCH :, :] = moved[0:EDGE, :]
    gz, _ = place()
    stiff = conf_ref[0].astype(jnp.float32) * 0.25 * mask_ref[0].astype(jnp.float32)
    stiff = stiff * (gz > 0).astype(jnp.float32)
    gap = jnp.zeros((1, 48), jnp.float32)
    stiff = jnp.concatenate([gap, gap[:, :16], stiff, stiff, gap], axis=1)
    stiff_ref[...] = pltpu.roll(stiff, gz * 16, 1)


def window_kernel(shifted_ref, kept_ref, sent_ref, stiff_ref, windows_ref, fixed_ref):
    gz, xy = place()
    odd = lax.rem(xy, 2)
    sign = 1 - 2 * odd
    target = lax.rem(gz + odd, 4)
    peaks = [jnp.where(odd > 0, sent_ref[i, 0], kept_ref[i, 0]) for i in range(2)]
    for j in range(COLS):
        down = EDGE + sign * peaks[0][0, j]
        right = REACH + sign * peaks[1][0, j]
        for k, (u, v) in enumerate(((0, 0), (1, 0), (-1, 0), (0, 1), (0, -1))):
            windows_ref[k, j] = shifted_ref[right + v, j, pl.ds(down + u, PATCH), :]
    gap = jnp.zeros((1, LANES - 2 * COLS), jnp.float32)
    flow = [peaks[0].astype(jnp.float32), peaks[1].astype(jnp.float32), gap]
    flow = jnp.concatenate(flow, axis=1)
    fixed_ref[...] = stiff_ref[...] + pltpu.roll(flow, target * 16, 1)


def correlate_kernel(windows_ref, got_ref, fixed_ref, out_ref):
    gz, xy = place()
    odd = lax.rem(xy, 2)
    sign = 1 - 2 * odd
    target = lax.rem(gz + odd, 4)
    sums = []
    for j in range(COLS):
        got = got_ref[0, :, j * PATCH : (j + 1) * PATCH].astype(jnp.float32)
        sums.append(
            [
                jnp.sum(
                    jnp.sum((windows_ref[k, j] * got).reshape(PATCH // 8, 8, LANES), axis=0),
                    axis=0,
                    keepdims=True,
                )
                for k in range(5)
            ]
        )
    scores = []
    for k in range(5):
        stacked = jnp.concatenate([sums[j][k] for j in range(COLS)], axis=0)
        scores.append(jnp.sum(stacked, axis=1, keepdims=True) * (1.0 / PATCH))
    center, y_plus, y_minus, x_plus, x_minus = scores
    scale = jnp.where(target > 0, sign, 0).astype(jnp.float32)
    delta_y = scale * (y_plus - y_minus) / (jnp.abs(y_minus) + jnp.abs(center) + jnp.abs(y_plus) + 1.0)
    delta_x = scale * (x_plus - x_minus) / (jnp.abs(x_minus) + jnp.abs(center) + jnp.abs(x_plus) + 1.0)
    lane = lax.broadcasted_iota(jnp.int32, (COLS, LANES), 1)
    patch = lax.broadcasted_iota(jnp.int32, (COLS, LANES), 0)
    spread = jnp.where(lane == target * 16 + patch, delta_y, 0.0)
    spread = spread + jnp.where(lane == target * 16 + COLS + patch, delta_x, 0.0)
    row = fixed_ref[...] + jnp.sum(spread, axis=0, keepdims=True)
    out_ref[...] = jnp.broadcast_to(row[None], out_ref.shape)


def relax_kernel(own_ref, got_ref, flow_ref, corr_ref):
    gz, xy = place()
    z = xy // PLANE
    inner = lax.rem(xy, PLANE)
    upper = inner < PLANE // 2

    own = own_ref[...]
    got = got_ref[...]
    window = jnp.concatenate([jnp.where(upper, got, own), jnp.where(upper, own, got)], axis=0)
    base = jnp.where(upper, z - 1, z) * PLANE
    here = jnp.where(upper, PLANE + inner, inner)
    shape = (2 * PLANE, LANES)
    lane = lax.broadcasted_iota(jnp.int32, shape, 1)
    local = lax.broadcasted_iota(jnp.int32, shape, 0)
    row = local + base
    col = lax.rem(lane, COLS)
    has_up = row > 0
    has_down = row < 63
    has_left = col > 0
    has_right = col < COLS - 1
    flow = jnp.where(lane < 64, window, 0.0)
    stiff = jnp.where(lane < 64, pltpu.roll(window, 64, 1), 0.0)
    next_stiff = jnp.where(lane < 48, pltpu.roll(window, 48, 1), 0.0)
    next_flow = jnp.where(lane < 48, pltpu.roll(window, LANES - 16, 1), 0.0)
    start = flow + jnp.where(lane >= 16, pltpu.roll(flow, 16, 1), 0.0)
    start = start + (
        jnp.where(lane >= 32, pltpu.roll(flow, 32, 1), 0.0)
        + jnp.where(lane >= 48, pltpu.roll(flow, 48, 1), 0.0)
    )
    nodes = start
    for _ in range(ITERS):
        rows = jnp.where(has_up, pltpu.roll(nodes, 1, 0) - nodes, 0.0)
        rows = rows + jnp.where(has_down, pltpu.roll(nodes, 2 * PLANE - 1, 0) - nodes, 0.0)
        cols = jnp.where(has_left, pltpu.roll(nodes, 1, 1) - nodes, 0.0)
        cols = cols + jnp.where(has_right, pltpu.roll(nodes, LANES - 1, 1) - nodes, 0.0)
        links = stiff * (pltpu.roll(nodes, 16, 1) + flow - nodes)
        links = links + next_stiff * (pltpu.roll(nodes, LANES - 16, 1) - next_flow - nodes)
        nodes = nodes + STEP_SIZE * ((rows + cols) + links)
    turn = lax.rem(LANES - gz * 16, LANES)
    for value, ref in ((flow, flow_ref), (nodes - start, corr_ref)):
        mine = jnp.sum(jnp.where(local == here, value, 0.0), axis=0, keepdims=True)
        mine = pltpu.roll(mine, turn, 1)
        ref[0, 0] = mine[:, 0:COLS]
        ref[1, 0] = mine[:, COLS : 2 * COLS]


def routes(groups, strips):
    last = strips // PLANE - 1
    swap, fetch, hop = [], [], []
    for group in range(groups):
        for strip in range(strips):
            this = group * strips + strip
            if strip % 2 == 0:
                swap.append((this, this + strips if group < groups - 1 else this + 1))
                fetch.append((this, group * strips + (strip ^ 2)))
            else:
                swap.append((this, this - strips if group > 0 else this - 1))
                fetch.append((this, (group - 1) % groups * strips + strip))
            plane, inner = divmod(strip, PLANE)
            twin = this ^ 1
            turn = this - inner + PLANE - 2 - inner // 2 * 2 + inner % 2
            if inner < PLANE // 2:
                hop.append((this, twin + PLANE if plane < last else turn))
            else:
                hop.append((this, twin - PLANE if plane > 0 else turn))
    return swap, fetch, hop


def on_device(sections, peak_offsets, confidence, tissue_mask):
    groups = lax.axis_size("gz")
    strips = lax.axis_size("xy")
    swap, fetch, hop = routes(groups, strips)
    got = lax.ppermute(sections, ("gz", "xy"), swap)
    sent = lax.ppermute(peak_offsets, ("gz", "xy"), fetch)
    vmem = pl.BlockSpec(memory_space=pltpu.VMEM)
    shifted, stiff, kept = pl.pallas_call(
        prepare_kernel,
        out_shape=(
            jax.ShapeDtypeStruct((2 * REACH + 1, COLS, PATCH + 2 * EDGE, LANES), jnp.float32),
            jax.ShapeDtypeStruct((1, LANES), jnp.float32),
            jax.ShapeDtypeStruct(peak_offsets.shape, jnp.int32),
        ),
        in_specs=[vmem, vmem, vmem, vmem],
        out_specs=(vmem, vmem, vmem),
        compiler_params=pltpu.CompilerParams(vmem_limit_bytes=8 * MIB),
    )(sections, peak_offsets, confidence, tissue_mask)
    windows, fixed = pl.pallas_call(
        window_kernel,
        out_shape=(
            jax.ShapeDtypeStruct((5, COLS, PATCH, LANES), jnp.float32),
            jax.ShapeDtypeStruct((1, LANES), jnp.float32),
        ),
        in_specs=[vmem, vmem, vmem, vmem],
        out_specs=(vmem, vmem),
        compiler_params=pltpu.CompilerParams(vmem_limit_bytes=8 * MIB),
    )(shifted, kept, sent, stiff)
    row = pl.pallas_call(
        correlate_kernel,
        out_shape=jax.ShapeDtypeStruct((32, 1, LANES), jnp.float32),
        in_specs=[vmem, vmem, vmem],
        out_specs=vmem,
        compiler_params=pltpu.CompilerParams(vmem_limit_bytes=8 * MIB),
    )(windows, got, fixed)
    planes = [
        [group * strips + plane * PLANE + inner for group in range(groups) for inner in range(PLANE)]
        for plane in range(strips // PLANE)
    ]
    block = lax.all_to_all(row, ("gz", "xy"), 0, 0, axis_index_groups=planes, tiled=True)
    block = jnp.sum(block.reshape(groups, PLANE, LANES), axis=0)
    beside = lax.ppermute(block, ("gz", "xy"), hop)
    shape = jax.ShapeDtypeStruct(peak_offsets.shape, jnp.float32)
    return pl.pallas_call(
        relax_kernel,
        out_shape=(shape, shape),
        in_specs=[vmem, vmem],
        out_specs=(vmem, vmem),
        compiler_params=pltpu.CompilerParams(vmem_limit_bytes=4 * MIB),
    )(block, beside)


def solution(mesh):
    in_specs = (
        P("gz", "xy", None),
        P(None, "gz", "xy", None),
        P("gz", "xy", None),
        P("gz", "xy", None),
    )
    out_specs = (P(None, "gz", "xy", None), P(None, "gz", "xy", None))
    return jax.shard_map(
        on_device, mesh=mesh, in_specs=in_specs, out_specs=out_specs, check_vma=False
    )
```

```python
import jax
import jax.numpy as jnp
from jax import lax
from jax.experimental import pallas as pl
from jax.experimental.pallas import tpu as pltpu
from jax.sharding import PartitionSpec as P

PATCH = 128
LANES = 128
COLS = 8
ITERS = 4
STEP_SIZE = 0.12
PLANE = 8
REACH = 3
EDGE = 8
MIB = 1024 * 1024


def place():
    gz = lax.axis_index("gz")
    xy = lax.axis_index("xy")
    return gz, xy


def prepare_kernel(own_ref, peak_ref, conf_ref, mask_ref, shifted_ref, stiff_ref, kept_ref):
    kept_ref[...] = peak_ref[...]
    for j in range(COLS):
        own = own_ref[0, :, j * PATCH : (j + 1) * PATCH].astype(jnp.float32)
        for v in range(2 * REACH + 1):
            moved = own if v == REACH else pltpu.roll(own, (REACH - v) % PATCH, 1)
            shifted_ref[v, j, EDGE : EDGE + PATCH, :] = moved
            shifted_ref[v, j, 0:EDGE, :] = moved[PATCH - EDGE :, :]
            shifted_ref[v, j, EDGE + PATCH :, :] = moved[0:EDGE, :]
    gz, _ = place()
    stiff = conf_ref[0].astype(jnp.float32) * 0.25 * mask_ref[0].astype(jnp.float32)
    stiff = stiff * (gz > 0).astype(jnp.float32)
    gap = jnp.zeros((1, 48), jnp.float32)
    stiff = jnp.concatenate([gap, gap[:, :16], stiff, stiff, gap], axis=1)
    stiff_ref[...] = pltpu.roll(stiff, gz * 16, 1)


def window_kernel(shifted_ref, kept_ref, sent_ref, stiff_ref, windows_ref, fixed_ref):
    gz, xy = place()
    odd = lax.rem(xy, 2)
    sign = 1 - 2 * odd
    target = lax.rem(gz + odd, 4)
    peaks = [jnp.where(odd > 0, sent_ref[i, 0], kept_ref[i, 0]) for i in range(2)]
    for j in range(COLS):
        down = EDGE + sign * peaks[0][0, j]
        right = REACH + sign * peaks[1][0, j]
        for k, (u, v) in enumerate(((0, 0), (1, 0), (-1, 0), (0, 1), (0, -1))):
            windows_ref[k, j] = shifted_ref[right + v, j, pl.ds(down + u, PATCH), :]
    flow = [peaks[0].astype(jnp.float32), peaks[1].astype(jnp.float32)] * 4
    flow = jnp.concatenate(flow + [jnp.zeros((1, LANES // 2), jnp.float32)], axis=1)
    lane = lax.broadcasted_iota(jnp.int32, (1, LANES), 1)
    fixed_ref[...] = stiff_ref[...] + jnp.where(lane >= target * 16, flow, 0.0)


def correlate_kernel(windows_ref, got_ref, fixed_ref, out_ref):
    gz, xy = place()
    odd = lax.rem(xy, 2)
    sign = 1 - 2 * odd
    target = lax.rem(gz + odd, 4)
    sums = []
    for j in range(COLS):
        got = got_ref[0, :, j * PATCH : (j + 1) * PATCH].astype(jnp.float32)
        sums.append(
            [
                jnp.sum(
                    jnp.sum((windows_ref[k, j] * got).reshape(PATCH // 8, 8, LANES), axis=0),
                    axis=0,
                    keepdims=True,
                )
                for k in range(5)
            ]
        )
    scores = []
    for k in range(5):
        stacked = jnp.concatenate([sums[j][k] for j in range(COLS)], axis=0)
        scores.append(jnp.sum(stacked, axis=1, keepdims=True) * (1.0 / PATCH))
    center, y_plus, y_minus, x_plus, x_minus = scores
    scale = jnp.where(target > 0, sign, 0).astype(jnp.float32)
    delta_y = scale * (y_plus - y_minus) / (jnp.abs(y_minus) + jnp.abs(center) + jnp.abs(y_plus) + 1.0)
    delta_x = scale * (x_plus - x_minus) / (jnp.abs(x_minus) + jnp.abs(center) + jnp.abs(x_plus) + 1.0)
    lane = lax.broadcasted_iota(jnp.int32, (COLS, LANES), 1)
    patch = lax.broadcasted_iota(jnp.int32, (COLS, LANES), 0)
    later = jnp.logical_and(lane >= target * 16, lane < 64)
    spread = jnp.where(lax.rem(lane, 16) == patch, delta_y, 0.0)
    spread = spread + jnp.where(lax.rem(lane, 16) == COLS + patch, delta_x, 0.0)
    spread = jnp.where(later, spread, 0.0)
    row = fixed_ref[...] + jnp.sum(spread, axis=0, keepdims=True)
    out_ref[...] = jnp.broadcast_to(row[None], out_ref.shape)


def relax_kernel(own_ref, got_ref, flow_ref, corr_ref):
    gz, xy = place()
    z = xy // PLANE
    inner = lax.rem(xy, PLANE)
    upper = inner < PLANE // 2

    own = own_ref[...]
    got = got_ref[...]
    window = jnp.concatenate([jnp.where(upper, got, own), jnp.where(upper, own, got)], axis=0)
    base = jnp.where(upper, z - 1, z) * PLANE
    here = jnp.where(upper, PLANE + inner, inner)
    shape = (2 * PLANE, LANES)
    lane = lax.broadcasted_iota(jnp.int32, shape, 1)
    local = lax.broadcasted_iota(jnp.int32, shape, 0)
    row = local + base
    col = lax.rem(lane, COLS)
    has_up = row > 0
    has_down = row < 63
    has_left = col > 0
    has_right = col < COLS - 1
    start = jnp.where(lane < 64, window, 0.0)
    stiff = STEP_SIZE * jnp.where(lane < 64, pltpu.roll(window, 64, 1), 0.0)
    next_stiff = STEP_SIZE * jnp.where(lane < 48, pltpu.roll(window, 48, 1), 0.0)
    flow = start - jnp.where(lane >= 16, pltpu.roll(start, 16, 1), 0.0)

    def neighbours(values):
        rows = jnp.where(has_up, pltpu.roll(values, 1, 0) - values, 0.0)
        rows = rows + jnp.where(has_down, pltpu.roll(values, 2 * PLANE - 1, 0) - values, 0.0)
        cols = jnp.where(has_left, pltpu.roll(values, 1, 1) - values, 0.0)
        cols = cols + jnp.where(has_right, pltpu.roll(values, LANES - 1, 1) - values, 0.0)
        return STEP_SIZE * (rows + cols)

    first = neighbours(start)
    moved = first
    for _ in range(ITERS - 1):
        links = stiff * (pltpu.roll(moved, 16, 1) - moved)
        links = links + next_stiff * (pltpu.roll(moved, LANES - 16, 1) - moved)
        moved = (moved + first) + (neighbours(moved) + links)
    turn = lax.rem(LANES - gz * 16, LANES)
    for value, ref in ((flow, flow_ref), (moved, corr_ref)):
        mine = jnp.sum(jnp.where(local == here, value, 0.0), axis=0, keepdims=True)
        mine = pltpu.roll(mine, turn, 1)
        ref[0, 0] = mine[:, 0:COLS]
        ref[1, 0] = mine[:, COLS : 2 * COLS]


def routes(groups, strips):
    last = strips // PLANE - 1
    swap, fetch, hop = [], [], []
    for group in range(groups):
        for strip in range(strips):
            this = group * strips + strip
            if strip % 2 == 0:
                swap.append((this, this + strips if group < groups - 1 else this + 1))
                fetch.append((this, group * strips + (strip ^ 2)))
            else:
                swap.append((this, this - strips if group > 0 else this - 1))
                fetch.append((this, (group - 1) % groups * strips + strip))
            plane, inner = divmod(strip, PLANE)
            twin = this ^ 1
            turn = this - inner + PLANE - 2 - inner // 2 * 2 + inner % 2
            if inner < PLANE // 2:
                hop.append((this, twin + PLANE if plane < last else turn))
            else:
                hop.append((this, twin - PLANE if plane > 0 else turn))
    return swap, fetch, hop


def on_device(sections, peak_offsets, confidence, tissue_mask):
    groups = lax.axis_size("gz")
    strips = lax.axis_size("xy")
    swap, fetch, hop = routes(groups, strips)
    got = lax.ppermute(sections, ("gz", "xy"), swap)
    sent = lax.ppermute(peak_offsets, ("gz", "xy"), fetch)
    vmem = pl.BlockSpec(memory_space=pltpu.VMEM)
    shifted, stiff, kept = pl.pallas_call(
        prepare_kernel,
        out_shape=(
            jax.ShapeDtypeStruct((2 * REACH + 1, COLS, PATCH + 2 * EDGE, LANES), jnp.float32),
            jax.ShapeDtypeStruct((1, LANES), jnp.float32),
            jax.ShapeDtypeStruct(peak_offsets.shape, jnp.int32),
        ),
        in_specs=[vmem, vmem, vmem, vmem],
        out_specs=(vmem, vmem, vmem),
        compiler_params=pltpu.CompilerParams(vmem_limit_bytes=8 * MIB),
    )(sections, peak_offsets, confidence, tissue_mask)
    windows, fixed = pl.pallas_call(
        window_kernel,
        out_shape=(
            jax.ShapeDtypeStruct((5, COLS, PATCH, LANES), jnp.float32),
            jax.ShapeDtypeStruct((1, LANES), jnp.float32),
        ),
        in_specs=[vmem, vmem, vmem, vmem],
        out_specs=(vmem, vmem),
        compiler_params=pltpu.CompilerParams(vmem_limit_bytes=8 * MIB),
    )(shifted, kept, sent, stiff)
    row = pl.pallas_call(
        correlate_kernel,
        out_shape=jax.ShapeDtypeStruct((32, 1, LANES), jnp.float32),
        in_specs=[vmem, vmem, vmem],
        out_specs=vmem,
        compiler_params=pltpu.CompilerParams(vmem_limit_bytes=8 * MIB),
    )(windows, got, fixed)
    planes = [
        [group * strips + plane * PLANE + inner for group in range(groups) for inner in range(PLANE)]
        for plane in range(strips // PLANE)
    ]
    block = lax.all_to_all(row, ("gz", "xy"), 0, 0, axis_index_groups=planes, tiled=True)
    block = jnp.sum(block.reshape(groups, PLANE, LANES), axis=0)
    beside = lax.ppermute(block, ("gz", "xy"), hop)
    shape = jax.ShapeDtypeStruct(peak_offsets.shape, jnp.float32)
    return pl.pallas_call(
        relax_kernel,
        out_shape=(shape, shape),
        in_specs=[vmem, vmem],
        out_specs=(vmem, vmem),
        compiler_params=pltpu.CompilerParams(vmem_limit_bytes=4 * MIB),
    )(block, beside)


def solution(mesh):
    in_specs = (
        P("gz", "xy", None),
        P(None, "gz", "xy", None),
        P("gz", "xy", None),
        P("gz", "xy", None),
    )
    out_specs = (P(None, "gz", "xy", None), P(None, "gz", "xy", None))
    return jax.shard_map(
        on_device, mesh=mesh, in_specs=in_specs, out_specs=out_specs, check_vma=False
    )
```

```python
import jax
import jax.numpy as jnp
from jax import lax
from jax.experimental import pallas as pl
from jax.experimental.pallas import tpu as pltpu
from jax.sharding import PartitionSpec as P

PATCH = 128
LANES = 128
COLS = 8
ITERS = 4
STEP_SIZE = 0.12
PLANE = 8
REACH = 3
EDGE = 8
MIB = 1024 * 1024


def place():
    gz = lax.axis_index("gz")
    xy = lax.axis_index("xy")
    return gz, xy


def prepare_kernel(own_ref, peak_ref, conf_ref, mask_ref, shifted_ref, stiff_ref, kept_ref):
    kept_ref[...] = peak_ref[...]
    for j in range(COLS):
        own = own_ref[0, :, j * PATCH : (j + 1) * PATCH].astype(jnp.float32)
        for v in range(2 * REACH + 1):
            moved = own if v == REACH else pltpu.roll(own, (REACH - v) % PATCH, 1)
            shifted_ref[v, j, EDGE : EDGE + PATCH, :] = moved
            shifted_ref[v, j, 0:EDGE, :] = moved[PATCH - EDGE :, :]
            shifted_ref[v, j, EDGE + PATCH :, :] = moved[0:EDGE, :]
    gz, _ = place()
    stiff = conf_ref[0].astype(jnp.float32) * 0.25 * mask_ref[0].astype(jnp.float32)
    stiff = stiff * (gz > 0).astype(jnp.float32)
    gap = jnp.zeros((1, 48), jnp.float32)
    stiff = jnp.concatenate([gap, gap[:, :16], stiff, stiff, gap], axis=1)
    stiff_ref[...] = pltpu.roll(stiff, gz * 16, 1)


def window_kernel(shifted_ref, kept_ref, sent_ref, stiff_ref, windows_ref, fixed_ref):
    gz, xy = place()
    odd = lax.rem(xy, 2)
    sign = 1 - 2 * odd
    target = lax.rem(gz + odd, 4)
    peaks = [jnp.where(odd > 0, sent_ref[i, 0], kept_ref[i, 0]) for i in range(2)]
    for j in range(COLS):
        down = EDGE + sign * peaks[0][0, j]
        right = REACH + sign * peaks[1][0, j]
        for k, (u, v) in enumerate(((0, 0), (1, 0), (-1, 0), (0, 1), (0, -1))):
            windows_ref[k, j] = shifted_ref[right + v, j, pl.ds(down + u, PATCH), :]
    flow = [peaks[0].astype(jnp.float32), peaks[1].astype(jnp.float32)] * 4
    flow = jnp.concatenate(flow + [jnp.zeros((1, LANES // 2), jnp.float32)], axis=1)
    lane = lax.broadcasted_iota(jnp.int32, (1, LANES), 1)
    fixed_ref[...] = stiff_ref[...] + jnp.where(lane >= target * 16, flow, 0.0)


def correlate_kernel(windows_ref, got_ref, fixed_ref, out_ref):
    gz, xy = place()
    odd = lax.rem(xy, 2)
    sign = 1 - 2 * odd
    target = lax.rem(gz + odd, 4)
    sums = []
    for j in range(COLS):
        got = got_ref[0, :, j * PATCH : (j + 1) * PATCH].astype(jnp.float32)
        sums.append(
            [
                jnp.sum(
                    jnp.sum((windows_ref[k, j] * got).reshape(PATCH // 8, 8, LANES), axis=0),
                    axis=0,
                    keepdims=True,
                )
                for k in range(5)
            ]
        )
    scores = []
    for k in range(5):
        stacked = jnp.concatenate([sums[j][k] for j in range(COLS)], axis=0)
        scores.append(jnp.sum(stacked, axis=1, keepdims=True) * (1.0 / PATCH))
    center, y_plus, y_minus, x_plus, x_minus = scores
    scale = jnp.where(target > 0, sign, 0).astype(jnp.float32)
    delta_y = scale * (y_plus - y_minus) / (jnp.abs(y_minus) + jnp.abs(center) + jnp.abs(y_plus) + 1.0)
    delta_x = scale * (x_plus - x_minus) / (jnp.abs(x_minus) + jnp.abs(center) + jnp.abs(x_plus) + 1.0)
    lane = lax.broadcasted_iota(jnp.int32, (COLS, LANES), 1)
    patch = lax.broadcasted_iota(jnp.int32, (COLS, LANES), 0)
    later = jnp.logical_and(lane >= target * 16, lane < 64)
    spread = jnp.where(lax.rem(lane, 16) == patch, delta_y, 0.0)
    spread = spread + jnp.where(lax.rem(lane, 16) == COLS + patch, delta_x, 0.0)
    spread = jnp.where(later, spread, 0.0)
    row = fixed_ref[...] + jnp.sum(spread, axis=0, keepdims=True)
    out_ref[...] = jnp.broadcast_to(row[None], out_ref.shape)


def put_row(value, hit, turn, ref):
    mine = jnp.sum(jnp.where(hit, value, 0.0), axis=0, keepdims=True)
    mine = pltpu.roll(mine, turn, 1)
    ref[0, 0] = mine[:, 0:COLS]
    ref[1, 0] = mine[:, COLS : 2 * COLS]


def flow_kernel(own_ref, flow_ref):
    gz, xy = place()
    lane = lax.broadcasted_iota(jnp.int32, (PLANE, LANES), 1)
    row = lax.broadcasted_iota(jnp.int32, (PLANE, LANES), 0)
    start = own_ref[...]
    flow = start - jnp.where(lane >= 16, pltpu.roll(start, 16, 1), 0.0)
    put_row(flow, row == lax.rem(xy, PLANE), lax.rem(LANES - gz * 16, LANES), flow_ref)


def relax_kernel(own_ref, got_ref, corr_ref):
    gz, xy = place()
    z = xy // PLANE
    inner = lax.rem(xy, PLANE)
    upper = inner < PLANE // 2

    own = own_ref[...]
    got = got_ref[...]
    window = jnp.concatenate([jnp.where(upper, got, own), jnp.where(upper, own, got)], axis=0)
    base = jnp.where(upper, z - 1, z) * PLANE
    here = jnp.where(upper, PLANE + inner, inner)
    shape = (2 * PLANE, LANES)
    lane = lax.broadcasted_iota(jnp.int32, shape, 1)
    local = lax.broadcasted_iota(jnp.int32, shape, 0)
    row = local + base
    col = lax.rem(lane, COLS)
    has_up = row > 0
    has_down = row < 63
    has_left = col > 0
    has_right = col < COLS - 1
    start = jnp.where(lane < 64, window, 0.0)
    stiff = STEP_SIZE * jnp.where(lane < 64, pltpu.roll(window, 64, 1), 0.0)
    next_stiff = STEP_SIZE * jnp.where(lane < 48, pltpu.roll(window, 48, 1), 0.0)

    def neighbours(values):
        rows = jnp.where(has_up, pltpu.roll(values, 1, 0) - values, 0.0)
        rows = rows + jnp.where(has_down, pltpu.roll(values, 2 * PLANE - 1, 0) - values, 0.0)
        cols = jnp.where(has_left, pltpu.roll(values, 1, 1) - values, 0.0)
        cols = cols + jnp.where(has_right, pltpu.roll(values, LANES - 1, 1) - values, 0.0)
        return STEP_SIZE * (rows + cols)

    first = neighbours(start)
    moved = first
    for _ in range(ITERS - 1):
        links = stiff * (pltpu.roll(moved, 16, 1) - moved)
        links = links + next_stiff * (pltpu.roll(moved, LANES - 16, 1) - moved)
        moved = (moved + first) + (neighbours(moved) + links)
    put_row(moved, local == here, lax.rem(LANES - gz * 16, LANES), corr_ref)


def routes(groups, strips):
    last = strips // PLANE - 1
    swap, fetch, hop = [], [], []
    for group in range(groups):
        for strip in range(strips):
            this = group * strips + strip
            if strip % 2 == 0:
                swap.append((this, this + strips if group < groups - 1 else this + 1))
                fetch.append((this, group * strips + (strip ^ 2)))
            else:
                swap.append((this, this - strips if group > 0 else this - 1))
                fetch.append((this, (group - 1) % groups * strips + strip))
            plane, inner = divmod(strip, PLANE)
            twin = this ^ 1
            turn = this - inner + PLANE - 2 - inner // 2 * 2 + inner % 2
            if inner < PLANE // 2:
                hop.append((this, twin + PLANE if plane < last else turn))
            else:
                hop.append((this, twin - PLANE if plane > 0 else turn))
    return swap, fetch, hop


def on_device(sections, peak_offsets, confidence, tissue_mask):
    groups = lax.axis_size("gz")
    strips = lax.axis_size("xy")
    swap, fetch, hop = routes(groups, strips)
    got = lax.ppermute(sections, ("gz", "xy"), swap)
    sent = lax.ppermute(peak_offsets, ("gz", "xy"), fetch)
    vmem = pl.BlockSpec(memory_space=pltpu.VMEM)
    shifted, stiff, kept = pl.pallas_call(
        prepare_kernel,
        out_shape=(
            jax.ShapeDtypeStruct((2 * REACH + 1, COLS, PATCH + 2 * EDGE, LANES), jnp.float32),
            jax.ShapeDtypeStruct((1, LANES), jnp.float32),
            jax.ShapeDtypeStruct(peak_offsets.shape, jnp.int32),
        ),
        in_specs=[vmem, vmem, vmem, vmem],
        out_specs=(vmem, vmem, vmem),
        compiler_params=pltpu.CompilerParams(vmem_limit_bytes=8 * MIB),
    )(sections, peak_offsets, confidence, tissue_mask)
    windows, fixed = pl.pallas_call(
        window_kernel,
        out_shape=(
            jax.ShapeDtypeStruct((5, COLS, PATCH, LANES), jnp.float32),
            jax.ShapeDtypeStruct((1, LANES), jnp.float32),
        ),
        in_specs=[vmem, vmem, vmem, vmem],
        out_specs=(vmem, vmem),
        compiler_params=pltpu.CompilerParams(vmem_limit_bytes=8 * MIB),
    )(shifted, kept, sent, stiff)
    row = pl.pallas_call(
        correlate_kernel,
        out_shape=jax.ShapeDtypeStruct((32, 1, LANES), jnp.float32),
        in_specs=[vmem, vmem, vmem],
        out_specs=vmem,
        compiler_params=pltpu.CompilerParams(vmem_limit_bytes=8 * MIB),
    )(windows, got, fixed)
    planes = [
        [group * strips + plane * PLANE + inner for group in range(groups) for inner in range(PLANE)]
        for plane in range(strips // PLANE)
    ]
    block = lax.all_to_all(row, ("gz", "xy"), 0, 0, axis_index_groups=planes, tiled=True)
    block = jnp.sum(block.reshape(groups, PLANE, LANES), axis=0)
    beside = lax.ppermute(block, ("gz", "xy"), hop)
    shape = jax.ShapeDtypeStruct(peak_offsets.shape, jnp.float32)
    flow = pl.pallas_call(
        flow_kernel,
        out_shape=shape,
        in_specs=[vmem],
        out_specs=vmem,
        compiler_params=pltpu.CompilerParams(vmem_limit_bytes=4 * MIB),
    )(block)
    correction = pl.pallas_call(
        relax_kernel,
        out_shape=shape,
        in_specs=[vmem, vmem],
        out_specs=vmem,
        compiler_params=pltpu.CompilerParams(vmem_limit_bytes=4 * MIB),
    )(block, beside)
    return flow, correction


def solution(mesh):
    in_specs = (
        P("gz", "xy", None),
        P(None, "gz", "xy", None),
        P("gz", "xy", None),
        P("gz", "xy", None),
    )
    out_specs = (P(None, "gz", "xy", None), P(None, "gz", "xy", None))
    return jax.shard_map(
        on_device, mesh=mesh, in_specs=in_specs, out_specs=out_specs, check_vma=False
    )
```

```python
import jax
import jax.numpy as jnp
from jax import lax
from jax.experimental import pallas as pl
from jax.experimental.pallas import tpu as pltpu
from jax.sharding import PartitionSpec as P

PATCH = 128
LANES = 128
COLS = 8
ITERS = 4
STEP_SIZE = 0.12
PLANE = 8
REACH = 3
EDGE = 8
MIB = 1024 * 1024


def place():
    gz = lax.axis_index("gz")
    xy = lax.axis_index("xy")
    return gz, xy


def prepare_kernel(own_ref, peak_ref, conf_ref, mask_ref, shifted_ref, stiff_ref, kept_ref):
    kept_ref[...] = peak_ref[...]
    for j in range(COLS):
        own = own_ref[0, :, j * PATCH : (j + 1) * PATCH].astype(jnp.float32)
        for v in range(2 * REACH + 1):
            moved = own if v == REACH else pltpu.roll(own, (REACH - v) % PATCH, 1)
            shifted_ref[v, j, EDGE : EDGE + PATCH, :] = moved
            shifted_ref[v, j, 0:EDGE, :] = moved[PATCH - EDGE :, :]
            shifted_ref[v, j, EDGE + PATCH :, :] = moved[0:EDGE, :]
    gz, _ = place()
    stiff = conf_ref[0].astype(jnp.float32) * 0.25 * mask_ref[0].astype(jnp.float32)
    stiff = stiff * (gz > 0).astype(jnp.float32)
    gap = jnp.zeros((1, 48), jnp.float32)
    stiff = jnp.concatenate([gap, gap[:, :16], stiff, stiff, gap], axis=1)
    stiff_ref[...] = pltpu.roll(stiff, gz * 16, 1)


def window_kernel(shifted_ref, kept_ref, sent_ref, stiff_ref, windows_ref, fixed_ref):
    gz, xy = place()
    odd = lax.rem(xy, 2)
    sign = 1 - 2 * odd
    target = lax.rem(gz + odd, 4)
    peaks = [jnp.where(odd > 0, sent_ref[i, 0], kept_ref[i, 0]) for i in range(2)]
    for j in range(COLS):
        down = EDGE + sign * peaks[0][0, j]
        right = REACH + sign * peaks[1][0, j]
        for k, (u, v) in enumerate(((0, 0), (1, 0), (-1, 0), (0, 1), (0, -1))):
            windows_ref[k, j] = shifted_ref[right + v, j, pl.ds(down + u, PATCH), :]
    flow = [peaks[0].astype(jnp.float32), peaks[1].astype(jnp.float32)] * 4
    flow = jnp.concatenate(flow + [jnp.zeros((1, LANES // 2), jnp.float32)], axis=1)
    lane = lax.broadcasted_iota(jnp.int32, (1, LANES), 1)
    fixed_ref[...] = stiff_ref[...] + jnp.where(lane >= target * 16, flow, 0.0)


def correlate_kernel(windows_ref, got_ref, fixed_ref, out_ref):
    gz, xy = place()
    odd = lax.rem(xy, 2)
    sign = 1 - 2 * odd
    target = lax.rem(gz + odd, 4)
    sums = []
    for j in range(COLS):
        got = got_ref[0, :, j * PATCH : (j + 1) * PATCH].astype(jnp.float32)
        sums.append(
            [
                jnp.sum(
                    jnp.sum((windows_ref[k, j] * got).reshape(PATCH // 8, 8, LANES), axis=0),
                    axis=0,
                    keepdims=True,
                )
                for k in range(5)
            ]
        )
    scores = []
    for k in range(5):
        stacked = jnp.concatenate([sums[j][k] for j in range(COLS)], axis=0)
        scores.append(jnp.sum(stacked, axis=1, keepdims=True) * (1.0 / PATCH))
    center, y_plus, y_minus, x_plus, x_minus = scores
    scale = jnp.where(target > 0, sign, 0).astype(jnp.float32)
    delta_y = scale * (y_plus - y_minus) / (jnp.abs(y_minus) + jnp.abs(center) + jnp.abs(y_plus) + 1.0)
    delta_x = scale * (x_plus - x_minus) / (jnp.abs(x_minus) + jnp.abs(center) + jnp.abs(x_plus) + 1.0)
    lane = lax.broadcasted_iota(jnp.int32, (COLS, LANES), 1)
    patch = lax.broadcasted_iota(jnp.int32, (COLS, LANES), 0)
    later = jnp.logical_and(lane >= target * 16, lane < 64)
    spread = jnp.where(lax.rem(lane, 16) == patch, delta_y, 0.0)
    spread = spread + jnp.where(lax.rem(lane, 16) == COLS + patch, delta_x, 0.0)
    spread = jnp.where(later, spread, 0.0)
    row = fixed_ref[...] + jnp.sum(spread, axis=0, keepdims=True)
    out_ref[...] = jnp.broadcast_to(row[None], out_ref.shape)


def put_row(value, index, lanes, ref):
    mine = pltpu.roll(value, lax.rem(PLANE - index, PLANE), 0)[0:1]
    ref[0, 0] = pltpu.roll(mine, lax.rem(LANES - lanes, LANES), 1)[:, 0:COLS]
    ref[1, 0] = pltpu.roll(mine, LANES - COLS - lanes, 1)[:, 0:COLS]


def flow_kernel(own_ref, flow_ref):
    gz, xy = place()
    lane = lax.broadcasted_iota(jnp.int32, (PLANE, LANES), 1)
    start = own_ref[...]
    flow = start - jnp.where(lane >= 16, pltpu.roll(start, 16, 1), 0.0)
    put_row(flow, lax.rem(xy, PLANE), gz * 16, flow_ref)


def relax_kernel(own_ref, got_ref, corr_ref):
    gz, xy = place()
    z = xy // PLANE
    inner = lax.rem(xy, PLANE)
    upper = inner < PLANE // 2

    own = own_ref[...]
    got = got_ref[...]
    window = jnp.concatenate([jnp.where(upper, got, own), jnp.where(upper, own, got)], axis=0)
    base = jnp.where(upper, z - 1, z) * PLANE
    shape = (2 * PLANE, LANES)
    lane = lax.broadcasted_iota(jnp.int32, shape, 1)
    local = lax.broadcasted_iota(jnp.int32, shape, 0)
    row = local + base
    col = lax.rem(lane, COLS)
    has_up = row > 0
    has_down = row < 63
    has_left = col > 0
    has_right = col < COLS - 1
    start = jnp.where(lane < 64, window, 0.0)
    stiff = STEP_SIZE * jnp.where(lane < 64, pltpu.roll(window, 64, 1), 0.0)
    next_stiff = STEP_SIZE * jnp.where(lane < 48, pltpu.roll(window, 48, 1), 0.0)

    def neighbours(values):
        rows = jnp.where(has_up, pltpu.roll(values, 1, 0) - values, 0.0)
        rows = rows + jnp.where(has_down, pltpu.roll(values, 2 * PLANE - 1, 0) - values, 0.0)
        cols = jnp.where(has_left, pltpu.roll(values, 1, 1) - values, 0.0)
        cols = cols + jnp.where(has_right, pltpu.roll(values, LANES - 1, 1) - values, 0.0)
        return STEP_SIZE * (rows + cols)

    first = neighbours(start)
    moved = first
    for _ in range(ITERS - 1):
        links = stiff * (pltpu.roll(moved, 16, 1) - moved)
        links = links + next_stiff * (pltpu.roll(moved, LANES - 16, 1) - moved)
        moved = (moved + first) + (neighbours(moved) + links)
    put_row(jnp.where(upper, moved[PLANE:], moved[:PLANE]), inner, gz * 16, corr_ref)


def routes(groups, strips):
    last = strips // PLANE - 1
    swap, fetch, hop = [], [], []
    for group in range(groups):
        for strip in range(strips):
            this = group * strips + strip
            if strip % 2 == 0:
                swap.append((this, this + strips if group < groups - 1 else this + 1))
                fetch.append((this, group * strips + (strip ^ 2)))
            else:
                swap.append((this, this - strips if group > 0 else this - 1))
                fetch.append((this, (group - 1) % groups * strips + strip))
            plane, inner = divmod(strip, PLANE)
            twin = this ^ 1
            turn = this - inner + PLANE - 2 - inner // 2 * 2 + inner % 2
            if inner < PLANE // 2:
                hop.append((this, twin + PLANE if plane < last else turn))
            else:
                hop.append((this, twin - PLANE if plane > 0 else turn))
    return swap, fetch, hop


def on_device(sections, peak_offsets, confidence, tissue_mask):
    groups = lax.axis_size("gz")
    strips = lax.axis_size("xy")
    swap, fetch, hop = routes(groups, strips)
    got = lax.ppermute(sections, ("gz", "xy"), swap)
    sent = lax.ppermute(peak_offsets, ("gz", "xy"), fetch)
    vmem = pl.BlockSpec(memory_space=pltpu.VMEM)
    shifted, stiff, kept = pl.pallas_call(
        prepare_kernel,
        out_shape=(
            jax.ShapeDtypeStruct((2 * REACH + 1, COLS, PATCH + 2 * EDGE, LANES), jnp.float32),
            jax.ShapeDtypeStruct((1, LANES), jnp.float32),
            jax.ShapeDtypeStruct(peak_offsets.shape, jnp.int32),
        ),
        in_specs=[vmem, vmem, vmem, vmem],
        out_specs=(vmem, vmem, vmem),
        compiler_params=pltpu.CompilerParams(vmem_limit_bytes=8 * MIB),
    )(sections, peak_offsets, confidence, tissue_mask)
    windows, fixed = pl.pallas_call(
        window_kernel,
        out_shape=(
            jax.ShapeDtypeStruct((5, COLS, PATCH, LANES), jnp.float32),
            jax.ShapeDtypeStruct((1, LANES), jnp.float32),
        ),
        in_specs=[vmem, vmem, vmem, vmem],
        out_specs=(vmem, vmem),
        compiler_params=pltpu.CompilerParams(vmem_limit_bytes=8 * MIB),
    )(shifted, kept, sent, stiff)
    row = pl.pallas_call(
        correlate_kernel,
        out_shape=jax.ShapeDtypeStruct((32, 1, LANES), jnp.float32),
        in_specs=[vmem, vmem, vmem],
        out_specs=vmem,
        compiler_params=pltpu.CompilerParams(vmem_limit_bytes=8 * MIB),
    )(windows, got, fixed)
    planes = [
        [group * strips + plane * PLANE + inner for group in range(groups) for inner in range(PLANE)]
        for plane in range(strips // PLANE)
    ]
    block = lax.all_to_all(row, ("gz", "xy"), 0, 0, axis_index_groups=planes, tiled=True)
    block = jnp.sum(block.reshape(groups, PLANE, LANES), axis=0)
    beside = lax.ppermute(block, ("gz", "xy"), hop)
    shape = jax.ShapeDtypeStruct(peak_offsets.shape, jnp.float32)
    flow = pl.pallas_call(
        flow_kernel,
        out_shape=shape,
        in_specs=[vmem],
        out_specs=vmem,
        compiler_params=pltpu.CompilerParams(vmem_limit_bytes=4 * MIB),
    )(block)
    correction = pl.pallas_call(
        relax_kernel,
        out_shape=shape,
        in_specs=[vmem, vmem],
        out_specs=vmem,
        compiler_params=pltpu.CompilerParams(vmem_limit_bytes=4 * MIB),
    )(block, beside)
    return flow, correction


def solution(mesh):
    in_specs = (
        P("gz", "xy", None),
        P(None, "gz", "xy", None),
        P("gz", "xy", None),
        P("gz", "xy", None),
    )
    out_specs = (P(None, "gz", "xy", None), P(None, "gz", "xy", None))
    return jax.shard_map(
        on_device, mesh=mesh, in_specs=in_specs, out_specs=out_specs, check_vma=False
    )
```

```python
import jax
import jax.numpy as jnp
from jax import lax
from jax.experimental import pallas as pl
from jax.experimental.pallas import tpu as pltpu
from jax.sharding import PartitionSpec as P

PATCH = 128
LANES = 128
COLS = 8
ITERS = 4
STEP_SIZE = 0.12
PLANE = 8
REACH = 3
EDGE = 8
MIB = 1024 * 1024


def place():
    gz = lax.axis_index("gz")
    xy = lax.axis_index("xy")
    return gz, xy


def prepare_kernel(own_ref, peak_ref, conf_ref, mask_ref, shifted_ref, stiff_ref, kept_ref):
    kept_ref[...] = peak_ref[...]
    for j in range(COLS):
        own = own_ref[0, :, j * PATCH : (j + 1) * PATCH].astype(jnp.float32)
        for v in range(2 * REACH + 1):
            moved = own if v == REACH else pltpu.roll(own, (REACH - v) % PATCH, 1)
            shifted_ref[v, j, EDGE : EDGE + PATCH, :] = moved
            shifted_ref[v, j, 0:EDGE, :] = moved[PATCH - EDGE :, :]
            shifted_ref[v, j, EDGE + PATCH :, :] = moved[0:EDGE, :]
    gz, _ = place()
    stiff = conf_ref[0].astype(jnp.float32) * 0.25 * mask_ref[0].astype(jnp.float32)
    stiff = stiff * (gz > 0).astype(jnp.float32)
    gap = jnp.zeros((1, 48), jnp.float32)
    stiff = jnp.concatenate([gap, gap[:, :16], stiff, stiff, gap], axis=1)
    stiff_ref[...] = pltpu.roll(stiff, gz * 16, 1)


def window_kernel(shifted_ref, kept_ref, sent_ref, stiff_ref, windows_ref, fixed_ref):
    gz, xy = place()
    odd = lax.rem(xy, 2)
    sign = 1 - 2 * odd
    target = lax.rem(gz + odd, 4)
    peaks = [jnp.where(odd > 0, sent_ref[i, 0], kept_ref[i, 0]) for i in range(2)]
    for j in range(COLS):
        down = EDGE + sign * peaks[0][0, j]
        right = REACH + sign * peaks[1][0, j]
        for k, (u, v) in enumerate(((0, 0), (1, 0), (-1, 0), (0, 1), (0, -1))):
            windows_ref[k, j] = shifted_ref[right + v, j, pl.ds(down + u, PATCH), :]
    flow = [peaks[0].astype(jnp.float32), peaks[1].astype(jnp.float32)] * 4
    flow = jnp.concatenate(flow + [jnp.zeros((1, LANES // 2), jnp.float32)], axis=1)
    lane = lax.broadcasted_iota(jnp.int32, (1, LANES), 1)
    fixed_ref[...] = stiff_ref[...] + jnp.where(lane >= target * 16, flow, 0.0)


def correlate_kernel(windows_ref, got_ref, fixed_ref, out_ref):
    gz, xy = place()
    odd = lax.rem(xy, 2)
    sign = 1 - 2 * odd
    target = lax.rem(gz + odd, 4)
    sums = []
    for j in range(COLS):
        got = got_ref[0, :, j * PATCH : (j + 1) * PATCH].astype(jnp.float32)
        sums.append(
            [
                jnp.sum(
                    jnp.sum((windows_ref[k, j] * got).reshape(PATCH // 8, 8, LANES), axis=0),
                    axis=0,
                    keepdims=True,
                )
                for k in range(5)
            ]
        )
    scores = []
    for k in range(5):
        stacked = jnp.concatenate([sums[j][k] for j in range(COLS)], axis=0)
        scores.append(jnp.sum(stacked, axis=1, keepdims=True) * (1.0 / PATCH))
    center, y_plus, y_minus, x_plus, x_minus = scores
    scale = jnp.where(target > 0, sign, 0).astype(jnp.float32)
    delta_y = scale * (y_plus - y_minus) / (jnp.abs(y_minus) + jnp.abs(center) + jnp.abs(y_plus) + 1.0)
    delta_x = scale * (x_plus - x_minus) / (jnp.abs(x_minus) + jnp.abs(center) + jnp.abs(x_plus) + 1.0)
    lane = lax.broadcasted_iota(jnp.int32, (COLS, LANES), 1)
    patch = lax.broadcasted_iota(jnp.int32, (COLS, LANES), 0)
    later = jnp.logical_and(lane >= target * 16, lane < 64)
    spread = jnp.where(lax.rem(lane, 16) == patch, delta_y, 0.0)
    spread = spread + jnp.where(lax.rem(lane, 16) == COLS + patch, delta_x, 0.0)
    spread = jnp.where(later, spread, 0.0)
    row = fixed_ref[...] + jnp.sum(spread, axis=0, keepdims=True)
    out_ref[...] = jnp.broadcast_to(row[None], out_ref.shape)


def relax_kernel(own_ref, got_ref, flow_ref, corr_ref):
    gz, xy = place()
    z = xy // PLANE
    inner = lax.rem(xy, PLANE)
    upper = inner < PLANE // 2

    own = own_ref[...]
    got = got_ref[...]
    window = jnp.concatenate([jnp.where(upper, got, own), jnp.where(upper, own, got)], axis=0)
    base = jnp.where(upper, z - 1, z) * PLANE
    shape = (2 * PLANE, LANES)
    lane = lax.broadcasted_iota(jnp.int32, shape, 1)
    local = lax.broadcasted_iota(jnp.int32, shape, 0)
    row = local + base
    col = lax.rem(lane, COLS)
    has_up = row > 0
    has_down = row < 63
    has_left = col > 0
    has_right = col < COLS - 1
    start = jnp.where(lane < 64, window, 0.0)
    stiff = STEP_SIZE * jnp.where(lane < 64, pltpu.roll(window, 64, 1), 0.0)
    next_stiff = STEP_SIZE * jnp.where(lane < 48, pltpu.roll(window, 48, 1), 0.0)
    flow = start - jnp.where(lane >= 16, pltpu.roll(start, 16, 1), 0.0)

    def neighbours(values):
        rows = jnp.where(has_up, pltpu.roll(values, 1, 0) - values, 0.0)
        rows = rows + jnp.where(has_down, pltpu.roll(values, 2 * PLANE - 1, 0) - values, 0.0)
        cols = jnp.where(has_left, pltpu.roll(values, 1, 1) - values, 0.0)
        cols = cols + jnp.where(has_right, pltpu.roll(values, LANES - 1, 1) - values, 0.0)
        return STEP_SIZE * (rows + cols)

    first = neighbours(start)
    moved = first
    for _ in range(ITERS - 1):
        links = stiff * (pltpu.roll(moved, 16, 1) - moved)
        links = links + next_stiff * (pltpu.roll(moved, LANES - 16, 1) - moved)
        moved = (moved + first) + (neighbours(moved) + links)
    for value, ref in ((flow, flow_ref), (moved, corr_ref)):
        mine = jnp.where(upper, value[PLANE:], value[:PLANE])
        mine = pltpu.roll(mine, lax.rem(PLANE - inner, PLANE), 0)[0:1]
        ref[0, 0] = pltpu.roll(mine, lax.rem(LANES - gz * 16, LANES), 1)[:, 0:COLS]
        ref[1, 0] = pltpu.roll(mine, LANES - COLS - gz * 16, 1)[:, 0:COLS]


def routes(groups, strips):
    last = strips // PLANE - 1
    swap, fetch, hop = [], [], []
    for group in range(groups):
        for strip in range(strips):
            this = group * strips + strip
            if strip % 2 == 0:
                swap.append((this, this + strips if group < groups - 1 else this + 1))
                fetch.append((this, group * strips + (strip ^ 2)))
            else:
                swap.append((this, this - strips if group > 0 else this - 1))
                fetch.append((this, (group - 1) % groups * strips + strip))
            plane, inner = divmod(strip, PLANE)
            twin = this ^ 1
            turn = this - inner + PLANE - 2 - inner // 2 * 2 + inner % 2
            if inner < PLANE // 2:
                hop.append((this, twin + PLANE if plane < last else turn))
            else:
                hop.append((this, twin - PLANE if plane > 0 else turn))
    return swap, fetch, hop


def on_device(sections, peak_offsets, confidence, tissue_mask):
    groups = lax.axis_size("gz")
    strips = lax.axis_size("xy")
    swap, fetch, hop = routes(groups, strips)
    got = lax.ppermute(sections, ("gz", "xy"), swap)
    sent = lax.ppermute(peak_offsets, ("gz", "xy"), fetch)
    vmem = pl.BlockSpec(memory_space=pltpu.VMEM)
    shifted, stiff, kept = pl.pallas_call(
        prepare_kernel,
        out_shape=(
            jax.ShapeDtypeStruct((2 * REACH + 1, COLS, PATCH + 2 * EDGE, LANES), jnp.float32),
            jax.ShapeDtypeStruct((1, LANES), jnp.float32),
            jax.ShapeDtypeStruct(peak_offsets.shape, jnp.int32),
        ),
        in_specs=[vmem, vmem, vmem, vmem],
        out_specs=(vmem, vmem, vmem),
        compiler_params=pltpu.CompilerParams(vmem_limit_bytes=8 * MIB),
    )(sections, peak_offsets, confidence, tissue_mask)
    windows, fixed = pl.pallas_call(
        window_kernel,
        out_shape=(
            jax.ShapeDtypeStruct((5, COLS, PATCH, LANES), jnp.float32),
            jax.ShapeDtypeStruct((1, LANES), jnp.float32),
        ),
        in_specs=[vmem, vmem, vmem, vmem],
        out_specs=(vmem, vmem),
        compiler_params=pltpu.CompilerParams(vmem_limit_bytes=8 * MIB),
    )(shifted, kept, sent, stiff)
    row = pl.pallas_call(
        correlate_kernel,
        out_shape=jax.ShapeDtypeStruct((32, 1, LANES), jnp.float32),
        in_specs=[vmem, vmem, vmem],
        out_specs=vmem,
        compiler_params=pltpu.CompilerParams(vmem_limit_bytes=8 * MIB),
    )(windows, got, fixed)
    planes = [
        [group * strips + plane * PLANE + inner for group in range(groups) for inner in range(PLANE)]
        for plane in range(strips // PLANE)
    ]
    block = lax.all_to_all(row, ("gz", "xy"), 0, 0, axis_index_groups=planes, tiled=True)
    block = jnp.sum(block.reshape(groups, PLANE, LANES), axis=0)
    beside = lax.ppermute(block, ("gz", "xy"), hop)
    shape = jax.ShapeDtypeStruct(peak_offsets.shape, jnp.float32)
    return pl.pallas_call(
        relax_kernel,
        out_shape=(shape, shape),
        in_specs=[vmem, vmem],
        out_specs=(vmem, vmem),
        compiler_params=pltpu.CompilerParams(vmem_limit_bytes=4 * MIB),
    )(block, beside)


def solution(mesh):
    in_specs = (
        P("gz", "xy", None),
        P(None, "gz", "xy", None),
        P("gz", "xy", None),
        P("gz", "xy", None),
    )
    out_specs = (P(None, "gz", "xy", None), P(None, "gz", "xy", None))
    return jax.shard_map(
        on_device, mesh=mesh, in_specs=in_specs, out_specs=out_specs, check_vma=False
    )
```

```python
import jax
import jax.numpy as jnp
from jax import lax
from jax.experimental import pallas as pl
from jax.experimental.pallas import tpu as pltpu
from jax.sharding import PartitionSpec as P

PATCH = 128
LANES = 128
COLS = 8
ITERS = 4
STEP_SIZE = 0.12
PLANE = 8
REACH = 3
EDGE = 8
MIB = 1024 * 1024


def place():
    gz = lax.axis_index("gz")
    xy = lax.axis_index("xy")
    return gz, xy


def prepare_kernel(own_ref, peak_ref, conf_ref, mask_ref, shifted_ref, stiff_ref, kept_ref):
    kept_ref[...] = peak_ref[...]
    for j in range(COLS):
        own = own_ref[0, :, j * PATCH : (j + 1) * PATCH].astype(jnp.float32)
        for v in range(2 * REACH + 1):
            moved = own if v == REACH else pltpu.roll(own, (REACH - v) % PATCH, 1)
            shifted_ref[v, j, EDGE : EDGE + PATCH, :] = moved
            shifted_ref[v, j, 0:EDGE, :] = moved[PATCH - EDGE :, :]
            shifted_ref[v, j, EDGE + PATCH :, :] = moved[0:EDGE, :]
    gz, _ = place()
    stiff = conf_ref[0].astype(jnp.float32) * 0.25 * mask_ref[0].astype(jnp.float32)
    stiff = stiff * (gz > 0).astype(jnp.float32)
    gap = jnp.zeros((1, 48), jnp.float32)
    stiff = jnp.concatenate([gap, gap[:, :16], stiff, stiff, gap], axis=1)
    stiff_ref[...] = pltpu.roll(stiff, gz * 16, 1)


def window_kernel(shifted_ref, kept_ref, sent_ref, stiff_ref, windows_ref, fixed_ref):
    gz, xy = place()
    odd = lax.rem(xy, 2)
    sign = 1 - 2 * odd
    target = lax.rem(gz + odd, 4)
    peaks = [jnp.where(odd > 0, sent_ref[i, 0], kept_ref[i, 0]) for i in range(2)]
    for j in range(COLS):
        down = EDGE + sign * peaks[0][0, j]
        right = REACH + sign * peaks[1][0, j]
        for k, (u, v) in enumerate(((0, 0), (1, 0), (-1, 0), (0, 1), (0, -1))):
            windows_ref[k, j] = shifted_ref[right + v, j, pl.ds(down + u, PATCH), :]
    flow = [peaks[0].astype(jnp.float32), peaks[1].astype(jnp.float32)] * 4
    flow = jnp.concatenate(flow + [jnp.zeros((1, LANES // 2), jnp.float32)], axis=1)
    lane = lax.broadcasted_iota(jnp.int32, (1, LANES), 1)
    fixed_ref[...] = stiff_ref[...] + jnp.where(lane >= target * 16, flow, 0.0)


def correlate_kernel(windows_ref, got_ref, fixed_ref, out_ref):
    gz, xy = place()
    odd = lax.rem(xy, 2)
    sign = 1 - 2 * odd
    target = lax.rem(gz + odd, 4)
    sums = []
    for j in range(COLS):
        got = got_ref[0, :, j * PATCH : (j + 1) * PATCH].astype(jnp.float32)
        sums.append(
            [
                jnp.sum(
                    jnp.sum((windows_ref[k, j] * got).reshape(PATCH // 8, 8, LANES), axis=0),
                    axis=0,
                    keepdims=True,
                )
                for k in range(5)
            ]
        )
    scores = []
    for k in range(5):
        stacked = jnp.concatenate([sums[j][k] for j in range(COLS)], axis=0)
        scores.append(jnp.sum(stacked, axis=1, keepdims=True) * (1.0 / PATCH))
    center, y_plus, y_minus, x_plus, x_minus = scores
    scale = jnp.where(target > 0, sign, 0).astype(jnp.float32)
    delta_y = scale * (y_plus - y_minus) / (jnp.abs(y_minus) + jnp.abs(center) + jnp.abs(y_plus) + 1.0)
    delta_x = scale * (x_plus - x_minus) / (jnp.abs(x_minus) + jnp.abs(center) + jnp.abs(x_plus) + 1.0)
    lane = lax.broadcasted_iota(jnp.int32, (COLS, LANES), 1)
    patch = lax.broadcasted_iota(jnp.int32, (COLS, LANES), 0)
    later = jnp.logical_and(lane >= target * 16, lane < 64)
    spread = jnp.where(lax.rem(lane, 16) == patch, delta_y, 0.0)
    spread = spread + jnp.where(lax.rem(lane, 16) == COLS + patch, delta_x, 0.0)
    spread = jnp.where(later, spread, 0.0)
    row = fixed_ref[...] + jnp.sum(spread, axis=0, keepdims=True)
    out_ref[...] = jnp.broadcast_to(row[None], out_ref.shape)


def relax_kernel(own_ref, got_ref, flow_ref, corr_ref):
    gz, xy = place()
    z = xy // PLANE
    inner = lax.rem(xy, PLANE)
    upper = inner < PLANE // 2

    own = own_ref[...]
    got = got_ref[...]
    window = jnp.concatenate([jnp.where(upper, got, own), jnp.where(upper, own, got)], axis=0)
    base = jnp.where(upper, z - 1, z) * PLANE
    here = jnp.where(upper, PLANE + inner, inner)
    shape = (2 * PLANE, LANES)
    lane = lax.broadcasted_iota(jnp.int32, shape, 1)
    local = lax.broadcasted_iota(jnp.int32, shape, 0)
    row = local + base
    col = lax.rem(lane, COLS)
    has_up = row > 0
    has_down = row < 63
    has_left = col > 0
    has_right = col < COLS - 1
    start = jnp.where(lane < 64, window, 0.0)
    stiff = STEP_SIZE * jnp.where(lane < 64, pltpu.roll(window, 64, 1), 0.0)
    next_stiff = STEP_SIZE * jnp.where(lane < 48, pltpu.roll(window, 48, 1), 0.0)
    flow = start - jnp.where(lane >= 16, pltpu.roll(start, 16, 1), 0.0)

    def neighbours(values):
        rows = jnp.where(has_up, pltpu.roll(values, 1, 0) - values, 0.0)
        rows = rows + jnp.where(has_down, pltpu.roll(values, 2 * PLANE - 1, 0) - values, 0.0)
        cols = jnp.where(has_left, pltpu.roll(values, 1, 1) - values, 0.0)
        cols = cols + jnp.where(has_right, pltpu.roll(values, LANES - 1, 1) - values, 0.0)
        return STEP_SIZE * (rows + cols)

    first = neighbours(start)
    moved = first
    sides = [jnp.where(has, STEP_SIZE, 0.0) for has in (has_up, has_down, has_left, has_right)]
    keep = 1.0 - ((sides[0] + sides[1]) + (sides[2] + sides[3]) + (stiff + next_stiff))
    for _ in range(ITERS - 1):
        rows = sides[0] * pltpu.roll(moved, 1, 0) + sides[1] * pltpu.roll(moved, 2 * PLANE - 1, 0)
        cols = sides[2] * pltpu.roll(moved, 1, 1) + sides[3] * pltpu.roll(moved, LANES - 1, 1)
        links = stiff * pltpu.roll(moved, 16, 1) + next_stiff * pltpu.roll(moved, LANES - 16, 1)
        moved = (keep * moved + first) + ((rows + cols) + links)
    turn = lax.rem(LANES - gz * 16, LANES)
    for value, ref in ((flow, flow_ref), (moved, corr_ref)):
        mine = jnp.sum(jnp.where(local == here, value, 0.0), axis=0, keepdims=True)
        mine = pltpu.roll(mine, turn, 1)
        ref[0, 0] = mine[:, 0:COLS]
        ref[1, 0] = mine[:, COLS : 2 * COLS]


def routes(groups, strips):
    last = strips // PLANE - 1
    swap, fetch, hop = [], [], []
    for group in range(groups):
        for strip in range(strips):
            this = group * strips + strip
            if strip % 2 == 0:
                swap.append((this, this + strips if group < groups - 1 else this + 1))
                fetch.append((this, group * strips + (strip ^ 2)))
            else:
                swap.append((this, this - strips if group > 0 else this - 1))
                fetch.append((this, (group - 1) % groups * strips + strip))
            plane, inner = divmod(strip, PLANE)
            twin = this ^ 1
            turn = this - inner + PLANE - 2 - inner // 2 * 2 + inner % 2
            if inner < PLANE // 2:
                hop.append((this, twin + PLANE if plane < last else turn))
            else:
                hop.append((this, twin - PLANE if plane > 0 else turn))
    return swap, fetch, hop


def on_device(sections, peak_offsets, confidence, tissue_mask):
    groups = lax.axis_size("gz")
    strips = lax.axis_size("xy")
    swap, fetch, hop = routes(groups, strips)
    got = lax.ppermute(sections, ("gz", "xy"), swap)
    sent = lax.ppermute(peak_offsets, ("gz", "xy"), fetch)
    vmem = pl.BlockSpec(memory_space=pltpu.VMEM)
    shifted, stiff, kept = pl.pallas_call(
        prepare_kernel,
        out_shape=(
            jax.ShapeDtypeStruct((2 * REACH + 1, COLS, PATCH + 2 * EDGE, LANES), jnp.float32),
            jax.ShapeDtypeStruct((1, LANES), jnp.float32),
            jax.ShapeDtypeStruct(peak_offsets.shape, jnp.int32),
        ),
        in_specs=[vmem, vmem, vmem, vmem],
        out_specs=(vmem, vmem, vmem),
        compiler_params=pltpu.CompilerParams(vmem_limit_bytes=8 * MIB),
    )(sections, peak_offsets, confidence, tissue_mask)
    windows, fixed = pl.pallas_call(
        window_kernel,
        out_shape=(
            jax.ShapeDtypeStruct((5, COLS, PATCH, LANES), jnp.float32),
            jax.ShapeDtypeStruct((1, LANES), jnp.float32),
        ),
        in_specs=[vmem, vmem, vmem, vmem],
        out_specs=(vmem, vmem),
        compiler_params=pltpu.CompilerParams(vmem_limit_bytes=8 * MIB),
    )(shifted, kept, sent, stiff)
    row = pl.pallas_call(
        correlate_kernel,
        out_shape=jax.ShapeDtypeStruct((32, 1, LANES), jnp.float32),
        in_specs=[vmem, vmem, vmem],
        out_specs=vmem,
        compiler_params=pltpu.CompilerParams(vmem_limit_bytes=8 * MIB),
    )(windows, got, fixed)
    planes = [
        [group * strips + plane * PLANE + inner for group in range(groups) for inner in range(PLANE)]
        for plane in range(strips // PLANE)
    ]
    block = lax.all_to_all(row, ("gz", "xy"), 0, 0, axis_index_groups=planes, tiled=True)
    block = jnp.sum(block.reshape(groups, PLANE, LANES), axis=0)
    beside = lax.ppermute(block, ("gz", "xy"), hop)
    shape = jax.ShapeDtypeStruct(peak_offsets.shape, jnp.float32)
    return pl.pallas_call(
        relax_kernel,
        out_shape=(shape, shape),
        in_specs=[vmem, vmem],
        out_specs=(vmem, vmem),
        compiler_params=pltpu.CompilerParams(vmem_limit_bytes=4 * MIB),
    )(block, beside)


def solution(mesh):
    in_specs = (
        P("gz", "xy", None),
        P(None, "gz", "xy", None),
        P("gz", "xy", None),
        P("gz", "xy", None),
    )
    out_specs = (P(None, "gz", "xy", None), P(None, "gz", "xy", None))
    return jax.shard_map(
        on_device, mesh=mesh, in_specs=in_specs, out_specs=out_specs, check_vma=False
    )
```
